32 devices in a mesh: gz: 4 (over y, core), ta: 8 (over z, x).
Axes of the slice: x: 2, y: 2, z: 4, core: 2. Of those that a mesh axis runs over, the one named last changes fastest.
Arguments:
- volume: bfloat16 [24, 24, 40, 3072], P('gz', None, None, 'ta'), may hold values from -6 to 6
- sketch_matrix: bfloat16 [3072, 256], P('ta'), may hold values from -0.875 to 0.875
- brain_voxels: int32 [14336], P('gz'), may hold values from 0 to 5759, as said below
Outputs:
- sketch: float32 [14336, 256], P(('gz', 'ta'))
The draws below stay inside these ranges and needn't reach their ends.
Inputs may be any that keep to these rules, and one draw needn't show every extreme that they name: `brain_voxels`: each slab's 3584 entries are distinct and increasing; the first is 0 and the last 5759.
All inputs are finite; a program needn't handle non-finite values.
Results may differ from the reference program's by a relative error of at most 0.0003.
Values may be sent and summed in bfloat16 or wider, within the bound.
No kernel may reach another device: no remote copies, remote signals or barrier semaphores. Data moves between devices by JAX's collectives and lax.ppermute only.
A program may use at most 64 MiB of HBM per device.

```python
import math
import jax
import jax.numpy as jnp
from jax import lax

RANK = 256
CZ = 6
XW = 24
YW = 40
MASKN = 3584
T_DEV = 384
NZ = 24
TIME = 3072
N_GZ = 4
N_TA = 8


def draw_brain_voxels(key, part):
    slab_cells = CZ * XW * YW

    def single_slab(slab_number):
        slab_key = jax.random.fold_in(key, slab_number)
        shuffled = jax.random.permutation(slab_key, slab_cells - 2) + 1
        chosen = jnp.sort(shuffled[:MASKN - 2]).astype(jnp.int32)
        return jnp.concatenate([jnp.zeros((1,), jnp.int32), chosen, jnp.full((1,), slab_cells - 1, jnp.int32)])
    return jax.vmap(single_slab)(jnp.arange(N_GZ, dtype=jnp.int32)).reshape(-1)


def block_scale(stream_key, shape, split, low, high):
    level = 1.0
    for dim, blocks in split:
        draws = jax.random.uniform(jax.random.fold_in(jax.random.fold_in(stream_key, 6), dim), (blocks,), jnp.float32, low / len(split), high / len(split))
        level = level * jnp.repeat(jnp.exp(draws), shape[dim] // blocks).reshape((-1,) + (1,) * (len(shape) - 1 - dim))
    return level


def bell_draw(rng, shape, width, limit, pieces=(), kind=jnp.bfloat16):
    result = width * jax.random.normal(rng, shape, jnp.float32)
    if pieces:
        result = result * block_scale(rng, shape, pieces, -0.22, 0.18)
    return jnp.clip(result, -limit, limit).astype(kind)


def setup_inputs(seed: int = 0) -> dict:
    key_list = jax.random.split(jax.random.key(seed), 4)
    return {
        "volume": bell_draw(key_list[0], (NZ, XW, YW, TIME), 1.0, 6.0, ((0, 4), (3, 8))),
        "sketch_matrix": bell_draw(key_list[1], (TIME, RANK), (TIME // 64) ** -0.5, 0.875, ((0, 8),)),
        "brain_voxels": draw_brain_voxels(jax.random.fold_in(key_list[3], 71), 0),
    }


def kernel_taps():
    sigma = 3.0 / (2.0 * math.sqrt(2.0 * math.log(2.0)))
    raw_taps = [math.exp(-0.5 * (shift_k - 2) ** 2 / sigma ** 2) for shift_k in range(5)]
    summed = sum(raw_taps)
    return [value_k / summed for value_k in raw_taps]

def smooth_along(source, axis_num, kernel):
    extent = source.shape[axis_num]
    widths = [(0, 0)] * source.ndim
    widths[axis_num] = (2, 2)
    padded = jnp.pad(source, widths)
    summed = jnp.zeros_like(source)
    for shift_k in range(5):
        summed = summed + kernel[shift_k] * lax.slice_in_dim(padded, shift_k, shift_k + extent, axis=axis_num)
    return summed

def reference(volume, sketch_matrix, brain_voxels):
    kernel = kernel_taps()
    slab_cells = CZ * XW * YW
    offsets = (jnp.arange(N_GZ, dtype=jnp.int32) * slab_cells)[:, None]
    row_index = (brain_voxels.reshape(N_GZ, MASKN) + offsets).reshape(-1)

    def time_block(step_index, summed):
        first_col = (step_index * T_DEV).astype(jnp.int32)
        signal = lax.dynamic_slice_in_dim(volume, first_col, T_DEV, axis=3).astype(jnp.float32)
        for axis_num in (0, 1, 2):
            signal = smooth_along(signal, axis_num, kernel)
        picked = signal.reshape(NZ * XW * YW, T_DEV)[row_index]
        weights = lax.dynamic_slice_in_dim(sketch_matrix, first_col, T_DEV, axis=0).astype(jnp.float32)
        return summed + jnp.dot(picked, weights, precision=lax.Precision.HIGHEST, preferred_element_type=jnp.float32)
    start_sum = jnp.zeros((N_GZ * MASKN, RANK), jnp.float32)
    return lax.fori_loop(0, N_TA, time_block, start_sum)
```

```python
import functools
import math

import jax
import jax.numpy as jnp
from jax import lax
from jax.experimental import pallas as pl
from jax.experimental.pallas import tpu as pltpu
from jax.sharding import PartitionSpec as P

LANES = 128
LEVELS = 32766.0
STEPS = 128.0
VMEM = pltpu.CompilerParams(vmem_limit_bytes=24 * 1024 * 1024)
F32 = jnp.float32
I16 = jnp.int16


def kernel_taps():
    sigma = 3.0 / (2.0 * math.sqrt(2.0 * math.log(2.0)))
    raw_taps = [math.exp(-0.5 * (shift_k - 2) ** 2 / sigma**2) for shift_k in range(5)]
    summed = sum(raw_taps)
    return [value_k / summed for value_k in raw_taps]


def pack_block(values, out, row):
    rows, cols = values.shape
    half = rows // 2
    codes = []
    for part in range(2):
        v = values[part * half : (part + 1) * half].reshape(half // 8, 8, cols)
        top = jnp.maximum(jnp.max(jnp.abs(v), axis=0), 1e-30)
        code = jnp.ceil(jnp.log2(top) * STEPS) + 1.0
        inverse = jnp.exp2(code * (-1.0 / STEPS)) * LEVELS
        q = jnp.round(v * inverse[None]).astype(jnp.int32)
        codes.append(code.astype(jnp.int32))
        out[row + part * half : row + (part + 1) * half, :] = q.reshape(half, cols).astype(I16)
    out[row + rows : row + rows + 16, :] = jnp.concatenate(codes, axis=0).astype(I16)


def unpack_scales(block, rows):
    codes = block[rows : rows + 16, :].astype(jnp.int32).astype(F32)
    return jnp.exp2(codes * (1.0 / STEPS)) * (1.0 / LEVELS)


def unpack_half(block, rows, part, scales):
    half = rows // 2
    q = block[part * half : (part + 1) * half, :].astype(jnp.int32).astype(F32)
    q = q.reshape(half // 8, 8, q.shape[-1]) * scales[part * 8 : part * 8 + 8][None]
    return q.reshape(half, q.shape[-1])


def edge_kernel(planes, cells, chunks, v_hbm, w_ref, *refs):
    outs, (buf, sem) = refs[: 2 * chunks], refs[2 * chunks :]
    odd = lax.axis_index("gz") % 2
    far = (planes - 2) * odd
    near = (planes - 2) * (1 - odd)
    copies = []
    for i, plane in enumerate((far, far + 1, near, near + 1)):
        rows = pl.ds(pl.multiple_of(plane * cells, cells), cells)
        copies.append(pltpu.make_async_copy(v_hbm.at[rows, :], buf.at[i], sem.at[i]))
        copies[-1].start()
    for i in range(4):
        copies[i].wait()
        product = jnp.dot(buf[i], w_ref[...], preferred_element_type=F32)
        for c in range(chunks):
            pack_block(
                product[:, c * LANES : (c + 1) * LANES],
                outs[2 * c + i // 2].at[i % 2],
                0,
            )


def slab_kernel(
    taps, shape, tile, share, chunk, v_hbm, w_ref, halo_ref, near_ref, bv_ref, first_ref,
    send_ref, keep_ref, buf, prod, pad, picked, sem,
):
    planes, width_x, width_y = shape
    cells = width_x * width_y
    blocks = send_ref.shape[0]
    window = tile + 8
    _, t1, t2 = taps[2], taps[1], taps[0]
    t0 = taps[2]
    copies = []
    for p in range(planes):
        rows = pl.ds(p * cells, cells)
        copies.append(pltpu.make_async_copy(v_hbm.at[rows, :], buf.at[p], sem.at[p]))
        copies[-1].start()
    odd = lax.axis_index("gz") % 2
    for ref, base in ((halo_ref, (planes + 2) * odd), (near_ref, (planes + 2) * (1 - odd))):
        for i in range(2):
            block = ref.at[i]
            scales = unpack_scales(block, cells)
            for part in range(2):
                half = cells // 2
                prod[base + i, part * half : (part + 1) * half, :] = unpack_half(
                    block, cells, part, scales
                )
    picked[...] = jnp.zeros_like(picked)
    pad[...] = jnp.zeros_like(pad)
    w = w_ref[:, chunk * LANES : (chunk + 1) * LANES]
    for p in range(planes):
        copies[p].wait()
        prod[p + 2] = jnp.dot(buf[p], w, preferred_element_type=F32)

    stride = width_y + 8
    per_tile = tile // width_y
    lane = lax.broadcasted_iota(jnp.int32, (window, LANES), 1)

    def plane_step(p, carry):
        def row(x):
            at = [prod[p + k, x * width_y : (x + 1) * width_y, :] for k in range(5)]
            return t0 * at[2] + t1 * (at[1] + at[3]) + t2 * (at[0] + at[4])

        zero = jnp.zeros((width_y, LANES), F32)
        win = [zero, zero, row(0), row(1)]
        for x in range(width_x):
            win.append(row(x + 2) if x + 2 < width_x else zero)
            value = t0 * win[2] + t1 * (win[1] + win[3]) + t2 * (win[0] + win[4])
            pad[8 + x * stride : 8 + x * stride + width_y, :] = value
            win = win[1:]
        for t in range(width_x // per_tile):
            rows = []
            for x in range(t * per_tile, (t + 1) * per_tile):
                at = [pad[6 + k + x * stride : 6 + k + x * stride + width_y, :] for k in range(5)]
                rows.append(t0 * at[2] + t1 * (at[1] + at[3]) + t2 * (at[0] + at[4]))
            value = jnp.concatenate(rows, axis=0)
            high = value.astype(jnp.bfloat16)
            low = (value - high.astype(F32)).astype(jnp.bfloat16)
            number = p * (width_x // per_tile) + t
            start = pl.multiple_of((first_ref[number] // 8) * 8, 8)
            voxel = bv_ref[pl.ds(start, window), :] - number * tile
            hits = []
            for left in range(0, tile, LANES):
                right = min(tile - left, LANES)
                hit = jnp.where(voxel == lane + left, 1.0, 0.0)
                hits.append(hit[:, :right].astype(jnp.bfloat16))
            choose = jnp.concatenate(hits, axis=1)
            both = jnp.concatenate([high, low], axis=1)
            out = jnp.dot(choose, both, preferred_element_type=F32)
            picked[pl.ds(start, window), :] += out[:, :LANES] + out[:, LANES:]
        return carry

    lax.fori_loop(0, planes, plane_step, 0)
    mine = lax.axis_index("ta") % 2
    for k in range(blocks):
        theirs_at = pl.multiple_of((2 * k + 1 - mine) * share, 8)
        mine_at = pl.multiple_of((2 * k + mine) * share, 8)
        pack_block(picked[pl.ds(theirs_at, share), :], send_ref.at[k], 0)
        keep_ref[k] = picked[pl.ds(mine_at, share), :]


def middle_kernel(share, got_ref, keep_ref, own_ref, *refs):
    msgs = refs
    blocks = got_ref.shape[0]
    z = lax.axis_index("ta") // 2

    def total(k):
        block = got_ref.at[k]
        scales = unpack_scales(block, share)
        rest = jnp.concatenate([unpack_half(block, share, part, scales) for part in range(2)], axis=0)
        return keep_ref[k] + rest

    own_ref[...] = total(z)
    for d in range(1, blocks):
        pack_block(total(z ^ d), msgs[d - 1], 0)


def last_kernel(share, chunks, blocks, *refs):
    out_ref = refs[-1]
    half = share // 2
    for c in range(chunks):
        own, msgs = refs[c * blocks], refs[c * blocks + 1 : (c + 1) * blocks]
        scales = [unpack_scales(m, share) for m in msgs]
        for part in range(2):
            rows = slice(part * half, (part + 1) * half)
            value = own[rows, :]
            for m, s in zip(msgs, scales):
                value = value + unpack_half(m, share, part, s)
            out_ref[rows, c * LANES : (c + 1) * LANES] = value


def shards(volume, sketch_matrix, brain_voxels):
    taps = kernel_taps()
    planes, width_x, width_y, time_local = volume.shape
    cells = width_x * width_y
    slab = planes * cells
    rank = sketch_matrix.shape[1]
    chunks = rank // LANES
    picks = brain_voxels.shape[0]
    n_gz, n_ta = lax.axis_size("gz"), lax.axis_size("ta")
    share = picks // n_ta
    blocks = n_ta // 2
    tile = 6 * width_y
    window = tile + 8
    tiles = slab // tile
    vmem = pl.BlockSpec(memory_space=pltpu.VMEM)
    smem = pl.BlockSpec(memory_space=pltpu.SMEM)
    hbm = pl.BlockSpec(memory_space=pl.ANY)
    flat = volume.reshape(slab, time_local)

    edge = pl.pallas_call(
        functools.partial(edge_kernel, planes, cells, chunks),
        out_shape=[jax.ShapeDtypeStruct((2, cells + 16, LANES), I16)] * (2 * chunks),
        in_specs=[hbm, vmem],
        out_specs=[vmem] * (2 * chunks),
        scratch_shapes=[
            pltpu.VMEM((4, cells, time_local), jnp.bfloat16),
            pltpu.SemaphoreType.DMA((4,)),
        ],
        compiler_params=VMEM,
        cost_estimate=pl.CostEstimate(
            flops=8 * cells * time_local * rank,
            bytes_accessed=8 * cells * (time_local + rank),
            transcendentals=0,
        ),
        name="edge_products",
    )(flat, sketch_matrix)

    even_pairs = [(i, i ^ 1) for i in range(n_gz)]
    odd_pairs = [(i, i + 1) for i in range(1, n_gz - 1, 2)]
    odd_pairs = odd_pairs + [(j, i) for i, j in odd_pairs]
    side = [(i, i ^ 1) for i in range(n_ta)]

    first = jnp.sum(
        brain_voxels[None, :] < (jnp.arange(tiles, dtype=jnp.int32) * tile)[:, None],
        axis=1,
        dtype=jnp.int32,
    )
    wide = jnp.broadcast_to(
        jnp.pad(brain_voxels, (0, window), constant_values=-1)[:, None], (picks + window, LANES)
    )

    results = []
    for c in range(chunks):
        halo = lax.ppermute(edge[2 * c], "gz", odd_pairs)
        near = lax.ppermute(edge[2 * c + 1], "gz", even_pairs)
        send, keep = pl.pallas_call(
            functools.partial(
                slab_kernel, taps, (planes, width_x, width_y), tile, share, c
            ),
            out_shape=[
                jax.ShapeDtypeStruct((blocks, share + 16, LANES), I16),
                jax.ShapeDtypeStruct((blocks, share, LANES), F32),
            ],
            in_specs=[hbm, vmem, vmem, vmem, vmem, smem],
            out_specs=[vmem, vmem],
            scratch_shapes=[
                pltpu.VMEM((planes, cells, time_local), jnp.bfloat16),
                pltpu.VMEM((planes + 4, cells, LANES), F32),
                pltpu.VMEM((width_x * (width_y + 8) + 8, LANES), F32),
                pltpu.VMEM((picks + window, LANES), F32),
                pltpu.SemaphoreType.DMA((planes,)),
            ],
            compiler_params=VMEM,
            cost_estimate=pl.CostEstimate(
                flops=2 * slab * LANES * (time_local + 2 * window),
                bytes_accessed=2 * slab * time_local + 2 * picks * LANES * 4,
                transcendentals=0,
            ),
            name="slab_rows",
        )(flat, sketch_matrix, halo, near, wide, first)
        got = lax.ppermute(send, "ta", side)
        mids = pl.pallas_call(
            functools.partial(middle_kernel, share),
            out_shape=[jax.ShapeDtypeStruct((share, LANES), F32)]
            + [jax.ShapeDtypeStruct((share + 16, LANES), I16)] * (blocks - 1),
            in_specs=[vmem, vmem],
            out_specs=[vmem] * blocks,
            compiler_params=VMEM,
            cost_estimate=pl.CostEstimate(
                flops=4 * picks * LANES, bytes_accessed=5 * picks * LANES, transcendentals=0
            ),
            name="middle_sums",
        )(got, keep)
        results.append(mids[0])
        for d in range(1, blocks):
            pairs = [(i, i ^ (2 * d)) for i in range(n_ta)]
            results.append(lax.ppermute(mids[d], "ta", pairs))

    return pl.pallas_call(
        functools.partial(last_kernel, share, chunks, blocks),
        out_shape=jax.ShapeDtypeStruct((share, rank), F32),
        in_specs=[vmem] * (chunks * blocks),
        out_specs=vmem,
        compiler_params=VMEM,
        name="last_sums",
    )(*results)


def solution(mesh):
    in_specs = (P("gz", None, None, "ta"), P("ta", None), P("gz"))
    out_specs = P(("gz", "ta"), None)
    return jax.shard_map(shards, mesh=mesh, in_specs=in_specs, out_specs=out_specs, check_vma=False)
```

```python
import functools
import math

import jax
import jax.numpy as jnp
from jax import lax
from jax.experimental import pallas as pl
from jax.experimental.pallas import tpu as pltpu
from jax.sharding import PartitionSpec as P

LANES = 128
LEVELS = 32766.0
STEPS = 128.0
VMEM = pltpu.CompilerParams(vmem_limit_bytes=24 * 1024 * 1024)
F32 = jnp.float32
I16 = jnp.int16


def kernel_taps():
    sigma = 3.0 / (2.0 * math.sqrt(2.0 * math.log(2.0)))
    raw_taps = [math.exp(-0.5 * (shift_k - 2) ** 2 / sigma**2) for shift_k in range(5)]
    summed = sum(raw_taps)
    return [value_k / summed for value_k in raw_taps]


def pack_block(values, out, row):
    rows, cols = values.shape
    half = rows // 2
    codes = []
    for part in range(2):
        v = values[part * half : (part + 1) * half].reshape(half // 8, 8, cols)
        top = jnp.maximum(jnp.max(jnp.abs(v), axis=0), 1e-30)
        code = jnp.ceil(jnp.log2(top) * STEPS) + 1.0
        inverse = jnp.exp2(code * (-1.0 / STEPS)) * LEVELS
        q = jnp.round(v * inverse[None]).astype(jnp.int32)
        codes.append(code.astype(jnp.int32))
        out[row + part * half : row + (part + 1) * half, :] = q.reshape(half, cols).astype(I16)
    out[row + rows : row + rows + 16, :] = jnp.concatenate(codes, axis=0).astype(I16)


def unpack_scales(block, rows):
    codes = block[rows : rows + 16, :].astype(jnp.int32).astype(F32)
    return jnp.exp2(codes * (1.0 / STEPS)) * (1.0 / LEVELS)


def unpack_half(block, rows, part, scales):
    half = rows // 2
    q = block[part * half : (part + 1) * half, :].astype(jnp.int32).astype(F32)
    q = q.reshape(half // 8, 8, q.shape[-1]) * scales[part * 8 : part * 8 + 8][None]
    return q.reshape(half, q.shape[-1])


def product_kernel(first, cells, chunks, v_hbm, w_hbm, *refs):
    starts = first(lax.axis_index("gz") % 2)
    scratch = refs[-4:]
    buf, wbuf, sem, wsem = scratch
    refs = refs[:-4]
    msgs, prods = refs[-2 * chunks : -chunks], refs[-chunks:]
    load_w = pltpu.make_async_copy(w_hbm, wbuf, wsem.at[0])
    load_w.start()
    copies, planes = [], []
    for pair, start in enumerate(starts):
        for i in range(2):
            plane = start + i
            rows = pl.ds(pl.multiple_of(plane * cells, cells), cells)
            number = 2 * pair + i
            copies.append(pltpu.make_async_copy(v_hbm.at[rows, :], buf.at[number], sem.at[number]))
            copies[-1].start()
            planes.append(plane)
    load_w.wait()
    for i, plane in enumerate(planes):
        copies[i].wait()
        product = jnp.dot(buf[i], wbuf[...], preferred_element_type=F32)
        for c in range(chunks):
            part = product[:, c * LANES : (c + 1) * LANES]
            prods[c][plane] = part
            if i < 2:
                pack_block(part, msgs[c].at[i], 0)


def slab_kernel(
    ratios, shape, tile, share, prod, halo_ref, near_ref, bv_ref, first_ref,
    send_ref, keep_ref, ext, pad, picked,
):
    planes, width_x, width_y = shape
    cells = width_x * width_y
    blocks = send_ref.shape[0]
    window = tile + 8
    r1, r2 = ratios
    odd = lax.axis_index("gz") % 2
    half = cells // 2
    for ref, base in ((halo_ref, 2 * odd), (near_ref, 2 * (1 - odd))):
        for i in range(2):
            block = ref.at[i]
            scales = unpack_scales(block, cells)
            for part in range(2):
                ext[base + i, part * half : (part + 1) * half, :] = unpack_half(
                    block, cells, part, scales
                )
    stride = width_y + 8
    for side in range(2):
        for x in range(width_x + 1):
            pad[side, x * stride : x * stride + 8, :] = jnp.zeros((8, LANES), F32)
    picked[0:8, :] = jnp.zeros((8, LANES), F32)
    per_tile = tile // width_y
    lane = lax.broadcasted_iota(jnp.int32, (window, LANES), 1)

    def blur(at):
        return at[2] + r1 * (at[1] + at[3]) + r2 * (at[0] + at[4])

    def source(p, rows):
        if p < 0:
            return ext[p + 2, rows, :]
        if p >= planes:
            return ext[p - planes + 2, rows, :]
        return prod[p, rows, :]

    for p in range(planes):
        side = p % 2

        def row(x):
            rows = slice(x * width_y, (x + 1) * width_y)
            return blur([source(p + k - 2, rows) for k in range(5)])

        zero = jnp.zeros((width_y, LANES), F32)
        win = [zero, zero, row(0), row(1)]
        for x in range(width_x):
            win.append(row(x + 2) if x + 2 < width_x else zero)
            pad[side, 8 + x * stride : 8 + x * stride + width_y, :] = blur(win)
            win = win[1:]
        found = []
        for t in range(width_x // per_tile):
            rows = []
            for x in range(t * per_tile, (t + 1) * per_tile):
                base = 6 + x * stride
                rows.append(blur([pad[side, base + k : base + k + width_y, :] for k in range(5)]))
            value = jnp.concatenate(rows, axis=0)
            high = value.astype(jnp.bfloat16)
            low = (value - high.astype(F32)).astype(jnp.bfloat16)
            number = p * (width_x // per_tile) + t
            start = pl.multiple_of((first_ref[number] // 8) * 8, 8)
            voxel = bv_ref[pl.ds(start, window), :]
            hits = []
            for left in range(0, tile, LANES):
                right = min(tile - left, LANES)
                hit = jnp.where(voxel == lane + (left + number * tile), 1.0, 0.0)
                hits.append(hit[:, :right].astype(jnp.bfloat16))
            choose = jnp.concatenate(hits, axis=1)
            both = jnp.concatenate([high, low], axis=1)
            out = jnp.dot(choose, both, preferred_element_type=F32)
            found.append((start, out[:, :LANES] + out[:, LANES:]))
        for start, out in found:
            picked[pl.ds(start, 8), :] += out[:8]
            picked[pl.ds(pl.multiple_of(start + 8, 8), window - 8), :] = out[8:]

    mine = lax.axis_index("ta") % 2
    for k in range(blocks):
        theirs_at = pl.multiple_of((2 * k + 1 - mine) * share, 8)
        mine_at = pl.multiple_of((2 * k + mine) * share, 8)
        pack_block(picked[pl.ds(theirs_at, share), :], send_ref.at[k], 0)
        keep_ref[k] = picked[pl.ds(mine_at, share), :]


def middle_kernel(share, got_ref, keep_ref, own_ref, *refs):
    msgs = refs
    blocks = got_ref.shape[0]
    z = lax.axis_index("ta") // 2

    def total(k):
        block = got_ref.at[k]
        scales = unpack_scales(block, share)
        rest = jnp.concatenate([unpack_half(block, share, part, scales) for part in range(2)], axis=0)
        return keep_ref[k] + rest

    own_ref[...] = total(z)
    for d in range(1, blocks):
        pack_block(total(z ^ d), msgs[d - 1], 0)


def last_kernel(scale, share, chunks, blocks, *refs):
    out_ref = refs[-1]
    half = share // 2
    for c in range(chunks):
        own, msgs = refs[c * blocks], refs[c * blocks + 1 : (c + 1) * blocks]
        scales = [unpack_scales(m, share) for m in msgs]
        for part in range(2):
            rows = slice(part * half, (part + 1) * half)
            value = own[rows, :]
            for m, s in zip(msgs, scales):
                value = value + unpack_half(m, share, part, s)
            out_ref[rows, c * LANES : (c + 1) * LANES] = value * scale


def shards(volume, sketch_matrix, brain_voxels):
    taps = kernel_taps()
    ratios = (taps[1] / taps[2], taps[0] / taps[2])
    planes, width_x, width_y, time_local = volume.shape
    cells = width_x * width_y
    slab = planes * cells
    rank = sketch_matrix.shape[1]
    chunks = rank // LANES
    picks = brain_voxels.shape[0]
    n_gz, n_ta = lax.axis_size("gz"), lax.axis_size("ta")
    share = picks // n_ta
    blocks = n_ta // 2
    tile = 6 * width_y
    window = tile + 8
    tiles = slab // tile
    vmem = pl.BlockSpec(memory_space=pltpu.VMEM)
    smem = pl.BlockSpec(memory_space=pltpu.SMEM)
    hbm = pl.BlockSpec(memory_space=pltpu.HBM)
    flat = volume.reshape(slab, time_local)

    def products(first, pairs, held):
        names = [jax.ShapeDtypeStruct((2, cells + 16, LANES), I16)] * chunks
        names += [jax.ShapeDtypeStruct((planes, cells, LANES), F32)] * chunks
        out = pl.pallas_call(
            functools.partial(product_kernel, first, cells, chunks),
            out_shape=names,
            in_specs=[hbm, hbm] + [hbm] * len(held),
            out_specs=[vmem] * (2 * chunks),
            input_output_aliases={2 + i: chunks + i for i in range(len(held))},
            scratch_shapes=[
                pltpu.VMEM((2 * pairs, cells, time_local), jnp.bfloat16),
                pltpu.VMEM((time_local, rank), jnp.bfloat16),
                pltpu.SemaphoreType.DMA((2 * pairs,)),
                pltpu.SemaphoreType.DMA((1,)),
            ],
            compiler_params=VMEM,
            cost_estimate=pl.CostEstimate(
                flops=4 * pairs * cells * time_local * rank,
                bytes_accessed=4 * pairs * cells * time_local,
                transcendentals=0,
            ),
        )(pltpu.with_memory_space_constraint(flat, pltpu.HBM), pltpu.with_memory_space_constraint(sketch_matrix, pltpu.HBM), *held)
        return out[:chunks], out[chunks:]

    far, prods = products(lambda odd: [(planes - 2) * odd], 1, [])
    middle = list(range(2, planes - 2, 2))
    near, prods = products(lambda odd: [(planes - 2) * (1 - odd)] + middle, 1 + len(middle), prods)

    even_pairs = [(i, i ^ 1) for i in range(n_gz)]
    odd_pairs = [(i, i + 1) for i in range(1, n_gz - 1, 2)]
    odd_pairs = odd_pairs + [(j, i) for i, j in odd_pairs]
    side = [(i, i ^ 1) for i in range(n_ta)]

    first = jnp.sum(
        brain_voxels[None, :] < (jnp.arange(tiles, dtype=jnp.int32) * tile)[:, None],
        axis=1,
        dtype=jnp.int32,
    )
    wide = jnp.broadcast_to(
        jnp.pad(brain_voxels, (0, window), constant_values=-1)[:, None], (picks + window, LANES)
    )

    results = []
    for c in range(chunks):
        halo = lax.ppermute(far[c], "gz", odd_pairs)
        beside = lax.ppermute(near[c], "gz", even_pairs)
        send, keep = pl.pallas_call(
            functools.partial(slab_kernel, ratios, (planes, width_x, width_y), tile, share),
            out_shape=[
                jax.ShapeDtypeStruct((blocks, share + 16, LANES), I16),
                jax.ShapeDtypeStruct((blocks, share, LANES), F32),
            ],
            in_specs=[vmem, vmem, vmem, vmem, smem],
            out_specs=[vmem, vmem],
            scratch_shapes=[
                pltpu.VMEM((4, cells, LANES), F32),
                pltpu.VMEM((2, width_x * (width_y + 8) + 8, LANES), F32),
                pltpu.VMEM((picks + window, LANES), F32),
            ],
            compiler_params=VMEM,
            cost_estimate=pl.CostEstimate(
                flops=4 * slab * LANES * window,
                bytes_accessed=4 * slab * LANES + 8 * picks * LANES,
                transcendentals=0,
            ),
            name="slab_rows",
        )(prods[c], halo, beside, wide, first)
        got = lax.ppermute(send, "ta", side)
        mids = pl.pallas_call(
            functools.partial(middle_kernel, share),
            out_shape=[jax.ShapeDtypeStruct((share, LANES), F32)]
            + [jax.ShapeDtypeStruct((share + 16, LANES), I16)] * (blocks - 1),
            in_specs=[vmem, vmem],
            out_specs=[vmem] * blocks,
            compiler_params=VMEM,
            cost_estimate=pl.CostEstimate(
                flops=4 * picks * LANES, bytes_accessed=5 * picks * LANES, transcendentals=0
            ),
            name="middle_sums",
        )(got, keep)
        results.append(mids[0])
        for d in range(1, blocks):
            pairs = [(i, i ^ (2 * d)) for i in range(n_ta)]
            results.append(lax.ppermute(mids[d], "ta", pairs))

    return pl.pallas_call(
        functools.partial(last_kernel, taps[2] ** 3, share, chunks, blocks),
        out_shape=jax.ShapeDtypeStruct((share, rank), F32),
        in_specs=[vmem] * (chunks * blocks),
        out_specs=vmem,
        compiler_params=VMEM,
        name="last_sums",
    )(*results)


def solution(mesh):
    in_specs = (P("gz", None, None, "ta"), P("ta", None), P("gz"))
    out_specs = P(("gz", "ta"), None)
    return jax.shard_map(shards, mesh=mesh, in_specs=in_specs, out_specs=out_specs, check_vma=False)
```

```python
import functools
import math

import jax
import jax.numpy as jnp
from jax import lax
from jax.experimental import pallas as pl
from jax.experimental.pallas import tpu as pltpu
from jax.sharding import PartitionSpec as P

LANES = 128
LEVELS = 32766.0
STEPS = 128.0
FAR_PARTS, NEAR_PARTS = 4, 2
VMEM = pltpu.CompilerParams(vmem_limit_bytes=24 * 1024 * 1024)
F32 = jnp.float32
I16 = jnp.int16


def kernel_taps():
    sigma = 3.0 / (2.0 * math.sqrt(2.0 * math.log(2.0)))
    raw_taps = [math.exp(-0.5 * (shift_k - 2) ** 2 / sigma**2) for shift_k in range(5)]
    summed = sum(raw_taps)
    return [value_k / summed for value_k in raw_taps]


def pack_block(values, out, parts=2):
    rows, cols = values.shape
    size = rows // parts
    codes = []
    for part in range(parts):
        v = values[part * size : (part + 1) * size].reshape(size // 8, 8, cols)
        top = jnp.maximum(jnp.max(jnp.abs(v), axis=0), 1e-30)
        code = jnp.ceil(jnp.log2(top) * STEPS) + 1.0
        inverse = jnp.exp2(code * (-1.0 / STEPS)) * LEVELS
        q = jnp.round(v * inverse[None]).astype(jnp.int32)
        codes.append(code.astype(jnp.int32))
        out[part * size : (part + 1) * size, :] = q.reshape(size, cols).astype(I16)
    out[rows : rows + 8 * parts, :] = jnp.concatenate(codes, axis=0).astype(I16)


def unpack_scales(block, rows, parts=2):
    codes = block[rows : rows + 8 * parts, :].astype(jnp.int32).astype(F32)
    return jnp.exp2(codes * (1.0 / STEPS)) * (1.0 / LEVELS)


def unpack_part(block, rows, part, scales, parts=2):
    size = rows // parts
    q = block[part * size : (part + 1) * size, :].astype(jnp.int32).astype(F32)
    q = q.reshape(size // 8, 8, q.shape[-1]) * scales[part * 8 : part * 8 + 8][None]
    return q.reshape(size, q.shape[-1])


def product_kernel(plan, cells, chunks, v_hbm, w_hbm, *refs):
    outs, (buf, wbuf, sem) = refs[:-3], refs[-3:]
    planes, packs = plan(lax.axis_index("gz") % 2)
    msgs, prods = outs[-chunks - len(packs) : -chunks], outs[-chunks:]
    load = pltpu.make_async_copy(w_hbm, wbuf, sem.at[len(planes)])
    load.start()
    copies = []
    for i, plane in enumerate(planes):
        rows = pl.ds(pl.multiple_of(plane * cells, cells), cells)
        copies.append(pltpu.make_async_copy(v_hbm.at[rows, :], buf.at[i], sem.at[i]))
        copies[-1].start()
    load.wait()
    for i, plane in enumerate(planes):
        copies[i].wait()
        product = jnp.dot(buf[i], wbuf[...], preferred_element_type=F32)
        for c in range(chunks):
            prods[c][plane] = product[:, c * LANES : (c + 1) * LANES]
    for msg, (c, plane, parts) in zip(msgs, packs):
        for i in range(2):
            pack_block(prods[c][plane + i], msg.at[i], parts)


def slab_kernel(
    ratios, shape, tile, share, halves, prod, halo_ref, near_ref, bv_ref, first_ref, *refs
):
    planes, width_x, width_y = shape
    cells = width_x * width_y
    sends, keeps, (ext, pad, picked) = refs[:2], refs[2:4], refs[4:]
    window = tile + 8
    r1, r2 = ratios
    odd = lax.axis_index("gz") % 2
    g, last = lax.axis_index("gz"), lax.axis_size("gz") - 1
    inside = jnp.where((g == 0) | (g == last), 0.0, 1.0)
    for ref, base, parts, factor in (
        (halo_ref, 2 * odd, FAR_PARTS, inside),
        (near_ref, 2 * (1 - odd), NEAR_PARTS, 1.0),
    ):
        size = cells // parts
        for i in range(2):
            block = ref.at[i]
            scales = unpack_scales(block, cells, parts) * factor
            for part in range(parts):
                ext[base + i, part * size : (part + 1) * size, :] = unpack_part(
                    block, cells, part, scales, parts
                )
    stride = width_y + 8
    for side in range(2):
        for x in range(width_x + 1):
            pad[side, x * stride : x * stride + 8, :] = jnp.zeros((8, LANES), F32)
    picked[0:8, :] = jnp.zeros((8, LANES), F32)
    per_tile = tile // width_y
    lane = lax.broadcasted_iota(jnp.int32, (window, LANES), 1)

    def blur(at):
        return at[2] + r1 * (at[1] + at[3]) + r2 * (at[0] + at[4])

    def source(p, rows):
        if p < 0:
            return ext[p + 2, rows, :]
        if p >= planes:
            return ext[p - planes + 2, rows, :]
        return prod[p, rows, :]

    for p in range(planes):
        side = p % 2

        def row(x):
            rows = slice(x * width_y, (x + 1) * width_y)
            return blur([source(p + k - 2, rows) for k in range(5)])

        zero = jnp.zeros((width_y, LANES), F32)
        win = [zero, zero, row(0), row(1)]
        for x in range(width_x):
            win.append(row(x + 2) if x + 2 < width_x else zero)
            pad[side, 8 + x * stride : 8 + x * stride + width_y, :] = blur(win)
            win = win[1:]
        found = []
        for t in range(width_x // per_tile):
            rows = []
            for x in range(t * per_tile, (t + 1) * per_tile):
                base = 6 + x * stride
                rows.append(blur([pad[side, base + k : base + k + width_y, :] for k in range(5)]))
            value = jnp.concatenate(rows, axis=0)
            high = value.astype(jnp.bfloat16)
            low = (value - high.astype(F32)).astype(jnp.bfloat16)
            number = p * (width_x // per_tile) + t
            start = pl.multiple_of((first_ref[number] // 8) * 8, 8)
            voxel = bv_ref[pl.ds(start, window), :]
            hits = []
            for left in range(0, tile, LANES):
                right = min(tile - left, LANES)
                hit = jnp.where(voxel == lane + (left + number * tile), 1.0, 0.0)
                hits.append(hit[:, :right].astype(jnp.bfloat16))
            choose = jnp.concatenate(hits, axis=1)
            both = jnp.concatenate([high, low], axis=1)
            out = jnp.dot(choose, both, preferred_element_type=F32)
            found.append((start, out[:, :LANES] + out[:, LANES:]))
        for start, out in found:
            picked[pl.ds(start, 8), :] += out[:8]
            picked[pl.ds(pl.multiple_of(start + 8, 8), window - 8), :] = out[8:]

    mine = lax.axis_index("ta") % 2
    z = lax.axis_index("ta") // 2
    for send, keep, half in zip(sends, keeps, halves):
        for k, d in enumerate(half):
            theirs_at = pl.multiple_of((2 * (z ^ d) + 1 - mine) * share, 8)
            mine_at = pl.multiple_of((2 * (z ^ d) + mine) * share, 8)
            pack_block(picked[pl.ds(theirs_at, share), :], send.at[k])
            keep[k] = picked[pl.ds(mine_at, share), :]


def unpack_block(block, rows):
    scales = unpack_scales(block, rows)
    return jnp.concatenate([unpack_part(block, rows, part, scales) for part in range(2)], axis=0)


def pass_kernel(share, got_ref, keep_ref, out_ref):
    for k in range(got_ref.shape[0]):
        pack_block(keep_ref[k] + unpack_block(got_ref.at[k], share), out_ref.at[k])


def join_kernel(share, got_ref, keep_ref, near_ref, keep_out, *send_out):
    count = got_ref.shape[0]
    for k in range(count):
        total = keep_ref[k] + unpack_block(got_ref.at[k], share)
        total = total + unpack_block(near_ref.at[k], share)
        if k % 2:
            pack_block(total, send_out[0].at[k // 2])
        else:
            keep_out[k // 2] = total


def fold_kernel(share, got_ref, keep_ref, keep_out, *send_out):
    for k in range(got_ref.shape[0]):
        total = keep_ref[k] + unpack_block(got_ref.at[k], share)
        if k % 2:
            pack_block(total, send_out[0].at[k // 2])
        else:
            keep_out[k // 2] = total


def last_kernel(scale, share, chunks, *refs):
    out_ref = refs[-1]
    for c in range(chunks):
        own, got = refs[2 * c : 2 * c + 2]
        value = own[0] + unpack_block(got.at[0], share)
        out_ref[:, c * LANES : (c + 1) * LANES] = value * scale


def shards(volume, sketch_matrix, brain_voxels):
    taps = kernel_taps()
    ratios = (taps[1] / taps[2], taps[0] / taps[2])
    planes, width_x, width_y, time_local = volume.shape
    cells = width_x * width_y
    slab = planes * cells
    rank = sketch_matrix.shape[1]
    chunks = rank // LANES
    picks = brain_voxels.shape[0]
    n_gz, n_ta = lax.axis_size("gz"), lax.axis_size("ta")
    share = picks // n_ta
    blocks = n_ta // 2
    tile = 6 * width_y
    window = tile + 8
    tiles = slab // tile
    vmem = pl.BlockSpec(memory_space=pltpu.VMEM)
    smem = pl.BlockSpec(memory_space=pltpu.SMEM)
    hbm = pl.BlockSpec(memory_space=pltpu.HBM)
    flat = volume.reshape(slab, time_local)

    def products(plan, count, which, held):
        shapes = []
        for c in which:
            for parts in (FAR_PARTS, NEAR_PARTS):
                shapes.append(jax.ShapeDtypeStruct((2, cells + 8 * parts, LANES), I16))
        messages = len(shapes)
        shapes += [jax.ShapeDtypeStruct((planes, cells, LANES), F32)] * chunks
        out = pl.pallas_call(
            functools.partial(product_kernel, plan, cells, chunks),
            out_shape=shapes,
            in_specs=[hbm, hbm] + [vmem] * len(held),
            out_specs=[vmem] * len(shapes),
            input_output_aliases={2 + i: messages + i for i in range(len(held))},
            scratch_shapes=[
                pltpu.VMEM((count, cells, time_local), jnp.bfloat16),
                pltpu.VMEM((time_local, rank), jnp.bfloat16),
                pltpu.SemaphoreType.DMA((count + 1,)),
            ],
            compiler_params=VMEM,
            cost_estimate=pl.CostEstimate(
                flops=2 * count * cells * time_local * rank,
                bytes_accessed=2 * count * cells * time_local,
                transcendentals=0,
            ),
            name="middle_products" if held else "edge_products",
        )(
            pltpu.with_memory_space_constraint(flat, pltpu.HBM),
            pltpu.with_memory_space_constraint(sketch_matrix, pltpu.HBM),
            *held,
        )
        return out[:messages], out[messages:]

    def packs_of(which, odd):
        top = planes - 2
        return [
            (c, plane, parts)
            for c in which
            for plane, parts in ((top * odd, FAR_PARTS), (top * (1 - odd), NEAR_PARTS))
        ]

    def edge_plan(odd):
        far, near = (planes - 2) * odd, (planes - 2) * (1 - odd)
        return [far, far + 1, near, near + 1], packs_of([0], odd)

    def middle_plan(odd):
        return list(range(2, planes - 2)), packs_of(range(1, chunks), odd)

    first_messages, prods = products(edge_plan, 4, [0], [])
    prods, brain_voxels = lax.optimization_barrier((prods, brain_voxels))
    first = jnp.sum(
        brain_voxels[None, :] < (jnp.arange(tiles, dtype=jnp.int32) * tile)[:, None],
        axis=1,
        dtype=jnp.int32,
    )
    wide = jnp.broadcast_to(
        jnp.pad(brain_voxels, (0, window), constant_values=-1)[:, None], (picks + window, LANES)
    )
    prods, wide, first = lax.optimization_barrier((prods, wide, first))
    later_messages, prods = products(middle_plan, planes - 4, range(1, chunks), prods)
    messages = list(first_messages) + list(later_messages)

    even_pairs = [(i, i ^ 1) for i in range(n_gz)]
    odd_pairs = []
    for i in range(n_gz):
        for j in range(n_ta):
            partner = (i, j ^ 2) if i in (0, n_gz - 1) else (i + 1 if i % 2 else i - 1, j)
            odd_pairs.append((i * n_ta + j, partner[0] * n_ta + partner[1]))

    halves = (range(1, blocks, 2), range(0, blocks, 2))

    def sums(kernel, count, args, name, keeps):
        shapes = [jax.ShapeDtypeStruct((count - count // 2, share, LANES), F32)] * keeps
        sent = count // 2 if keeps else count
        if sent:
            shapes.append(jax.ShapeDtypeStruct((sent, share + 16, LANES), I16))
        return pl.pallas_call(
            functools.partial(kernel, share),
            out_shape=shapes,
            in_specs=[vmem] * len(args),
            out_specs=[vmem] * len(shapes),
            compiler_params=VMEM,
            cost_estimate=pl.CostEstimate(
                flops=4 * count * share * LANES,
                bytes_accessed=8 * count * share * LANES,
                transcendentals=0,
            ),
            name=name,
        )(*args)

    def across(value, mask):
        return lax.ppermute(value, "ta", [(i, i ^ mask) for i in range(n_ta)])

    results = []
    for c in range(chunks):
        near = lax.ppermute(messages[2 * c + 1], "gz", even_pairs)
        far = lax.ppermute(messages[2 * c], ("gz", "ta"), odd_pairs)
        rows = pl.pallas_call(
            functools.partial(
                slab_kernel, ratios, (planes, width_x, width_y), tile, share, halves
            ),
            out_shape=[
                jax.ShapeDtypeStruct((len(half), share + 16, LANES), I16) for half in halves
            ]
            + [jax.ShapeDtypeStruct((len(half), share, LANES), F32) for half in halves],
            in_specs=[vmem, vmem, vmem, vmem, smem],
            out_specs=[vmem] * 4,
            scratch_shapes=[
                pltpu.VMEM((4, cells, LANES), F32),
                pltpu.VMEM((2, width_x * (width_y + 8) + 8, LANES), F32),
                pltpu.VMEM((picks + window, LANES), F32),
            ],
            compiler_params=VMEM,
            cost_estimate=pl.CostEstimate(
                flops=4 * slab * LANES * window,
                bytes_accessed=4 * slab * LANES + 8 * picks * LANES,
                transcendentals=0,
            ),
            name="slab_rows",
        )(prods[c], far, near, wide, first)
        near_rows, kept_rows, near_keep, kept_keep = rows
        side_near, side_kept = across(near_rows, 1), across(kept_rows, 1)
        (out,) = sums(pass_kernel, blocks // 2, (side_near, near_keep), "pass_sums", 0)
        near_got = across(out, 2)
        count, mask = blocks // 2, 4
        keep, out = sums(join_kernel, count, (side_kept, kept_keep, near_got), "join_sums", 1)
        while count > 2:
            count //= 2
            keep, out = sums(fold_kernel, count, (across(out, mask), keep), "fold_sums", 1)
            mask *= 2
        results += [keep, across(out, mask)]

    return pl.pallas_call(
        functools.partial(last_kernel, taps[2] ** 3, share, chunks),
        out_shape=jax.ShapeDtypeStruct((share, rank), F32),
        in_specs=[vmem] * (2 * chunks),
        out_specs=vmem,
        compiler_params=VMEM,
        name="last_sums",
    )(*results)


def solution(mesh):
    in_specs = (P("gz", None, None, "ta"), P("ta", None), P("gz"))
    out_specs = P(("gz", "ta"), None)
    return jax.shard_map(shards, mesh=mesh, in_specs=in_specs, out_specs=out_specs, check_vma=False)
```

```python
import functools
import math

import jax
import jax.numpy as jnp
from jax import lax
from jax.experimental import pallas as pl
from jax.experimental.pallas import tpu as pltpu
from jax.sharding import PartitionSpec as P

LANES = 128
LEVELS = 32766.0
STEPS = 128.0
FAR_PARTS, NEAR_PARTS = 4, 2
VMEM = pltpu.CompilerParams(vmem_limit_bytes=24 * 1024 * 1024)
COST = pl.CostEstimate(flops=0, bytes_accessed=0, transcendentals=0)
F32 = jnp.float32
I16 = jnp.int16


def kernel_taps():
    sigma = 3.0 / (2.0 * math.sqrt(2.0 * math.log(2.0)))
    raw_taps = [math.exp(-0.5 * (shift_k - 2) ** 2 / sigma**2) for shift_k in range(5)]
    summed = sum(raw_taps)
    return [value_k / summed for value_k in raw_taps]


def pack_block(values, out, parts=2):
    rows, cols = values.shape
    size = rows // parts
    codes = []
    for part in range(parts):
        v = values[part * size : (part + 1) * size].reshape(size // 8, 8, cols)
        top = jnp.maximum(jnp.max(jnp.abs(v), axis=0), 1e-30)
        code = jnp.ceil(jnp.log2(top) * STEPS) + 1.0
        inverse = jnp.exp2(code * (-1.0 / STEPS)) * LEVELS
        q = jnp.round(v * inverse[None]).astype(jnp.int32)
        codes.append(code.astype(jnp.int32))
        out[part * size : (part + 1) * size, :] = q.reshape(size, cols).astype(I16)
    out[rows : rows + 8 * parts, :] = jnp.concatenate(codes, axis=0).astype(I16)


def unpack_scales(block, rows, parts=2):
    codes = block[rows : rows + 8 * parts, :].astype(jnp.int32).astype(F32)
    return jnp.exp2(codes * (1.0 / STEPS)) * (1.0 / LEVELS)


def unpack_part(block, rows, part, scales, parts=2):
    size = rows // parts
    q = block[part * size : (part + 1) * size, :].astype(jnp.int32).astype(F32)
    q = q.reshape(size // 8, 8, q.shape[-1]) * scales[part * 8 : part * 8 + 8][None]
    return q.reshape(size, q.shape[-1])


def product_kernel(plan, pack_first, cells, chunks, v_hbm, w_hbm, *refs):
    outs, (buf, wbuf, sem) = refs[:-3], refs[-3:]
    planes, packs = plan(lax.axis_index("gz") % 2)
    msgs, prods = outs[: len(packs)], outs[len(packs) :]
    load = pltpu.make_async_copy(w_hbm, wbuf, sem.at[len(planes)])
    load.start()
    copies = []
    for i, plane in enumerate(planes):
        rows = pl.ds(pl.multiple_of(plane * cells, cells), cells)
        copies.append(pltpu.make_async_copy(v_hbm.at[rows, :], buf.at[i], sem.at[i]))
        copies[-1].start()

    def pack():
        for msg, (c, plane, parts) in zip(msgs, packs):
            for i in range(2):
                pack_block(prods[c][plane + 2 + i], msg.at[i], parts)

    if pack_first:
        pack()
    load.wait()
    for i, plane in enumerate(planes):
        copies[i].wait()
        product = jnp.dot(buf[i], wbuf[...], preferred_element_type=F32)
        for c in range(chunks):
            prods[c][plane + 2] = product[:, c * LANES : (c + 1) * LANES]
    if not pack_first:
        pack()


def unpack_planes(ref, prod, slot, cells, parts, factor):
    size = cells // parts
    for i in range(2):
        block = ref.at[i]
        scales = unpack_scales(block, cells, parts) * factor
        for part in range(parts):
            prod[slot + i, part * size : (part + 1) * size, :] = unpack_part(
                block, cells, part, scales, parts
            )


def smooth_and_pick(ratios, shape, tile, prod, bv_ref, first_ref, pad, first_plane, count, write):
    width_x, width_y = shape
    window = tile + 8
    r1, r2 = ratios
    stride = width_y + 8
    for side in range(2):
        for x in range(width_x + 1):
            pad[side, x * stride : x * stride + 8, :] = jnp.zeros((8, LANES), F32)
    per_tile = tile // width_y
    tiles = width_x // per_tile
    lane = lax.broadcasted_iota(jnp.int32, (window, LANES), 1)

    def blur(at):
        return at[2] + r1 * (at[1] + at[3]) + r2 * (at[0] + at[4])

    for i in range(count):
        side = i % 2
        p = first_plane + i

        def row(x):
            rows = slice(x * width_y, (x + 1) * width_y)
            return blur([prod[p + k, rows, :] for k in range(5)])

        zero = jnp.zeros((width_y, LANES), F32)
        win = [zero, zero, row(0), row(1)]
        for x in range(width_x):
            win.append(row(x + 2) if x + 2 < width_x else zero)
            pad[side, 8 + x * stride : 8 + x * stride + width_y, :] = blur(win)
            win = win[1:]
        found = []
        for t in range(tiles):
            rows = []
            for x in range(t * per_tile, (t + 1) * per_tile):
                base = 6 + x * stride
                rows.append(blur([pad[side, base + k : base + k + width_y, :] for k in range(5)]))
            value = jnp.concatenate(rows, axis=0)
            high = value.astype(jnp.bfloat16)
            low = (value - high.astype(F32)).astype(jnp.bfloat16)
            number = p * tiles + t
            start = pl.multiple_of((first_ref[number] // 8) * 8, 8)
            voxel = bv_ref[pl.ds(start, window), :]
            hits = []
            for left in range(0, tile, LANES):
                right = min(tile - left, LANES)
                hit = jnp.where(voxel == lane + (left + number * tile), 1.0, 0.0)
                hits.append(hit[:, :right].astype(jnp.bfloat16))
            choose = jnp.concatenate(hits, axis=1)
            both = jnp.concatenate([high, low], axis=1)
            out = jnp.dot(choose, both, preferred_element_type=F32)
            found.append((start, out[:, :LANES] + out[:, LANES:]))
        for start, out in found:
            write(start, out)


def inner_kernel(ratios, shape, planes, tile, near_ref, bv_ref, first_ref, prod, picked, pad):
    odd = lax.axis_index("gz") % 2
    unpack_planes(near_ref, prod, (planes + 2) * (1 - odd), shape[0] * shape[1], NEAR_PARTS, 1.0)
    picked[...] = jnp.zeros_like(picked)

    def write(start, out):
        rest = out.shape[0] - 8
        picked[pl.ds(start, 8), :] += out[:8]
        picked[pl.ds(pl.multiple_of(start + 8, 8), rest), :] = out[8:]

    smooth_and_pick(
        ratios, shape, tile, prod, bv_ref, first_ref, pad, 2 * (1 - odd), planes - 2, write
    )


def middle_inner_kernel(
    ratios, shape, planes, tile, plan, chunks, v_hbm, w_hbm, near_ref, bv_ref, first_ref, *refs
):
    outs, (pad, buf, wbuf, sem) = refs[chunks:-4], refs[-4:]
    picked, msgs, prods = outs[0], outs[1:-chunks], outs[-chunks:]
    cells = shape[0] * shape[1]
    product_kernel(plan, True, cells, chunks, v_hbm, w_hbm, *msgs, *prods, buf, wbuf, sem)
    inner_kernel(
        ratios, shape, planes, tile, near_ref, bv_ref, first_ref, prods[0], picked, pad
    )


def later_inner_kernel(ratios, shape, planes, tile, _, near_ref, bv_ref, first_ref, *refs):
    inner_kernel(ratios, shape, planes, tile, near_ref, bv_ref, first_ref, *refs)


def outer_kernel(
    ratios, shape, planes, tile, share, pieces, carries, *refs
):
    _, far_ref, _, bv_ref, first_ref = refs[:5]
    carried, refs = refs[5 : 5 + carries], refs[5 + carries :]
    prod, picked, refs, pad = refs[0], refs[1], refs[2:-1], refs[-1]
    sends, keeps = refs[: len(pieces)], refs[len(pieces) :]
    g, last = lax.axis_index("gz"), lax.axis_size("gz") - 1
    odd = g % 2
    inside = jnp.where((g == 0) | (g == last), 0.0, 1.0)
    unpack_planes(far_ref, prod, (planes + 2) * odd, shape[0] * shape[1], FAR_PARTS, inside)

    def write(start, out):
        picked[pl.ds(start, out.shape[0]), :] += out

    smooth_and_pick(
        ratios, shape, tile, prod, bv_ref, first_ref, pad, (planes - 2) * odd, 2, write
    )
    mine = lax.axis_index("ta") % 2
    z = lax.axis_index("ta") // 2
    for send, keep, piece in zip(sends, keeps, pieces):
        skip = send.shape[0] - len(piece)
        for k in range(skip):
            send[k] = carried[k][0]
        for k, d in enumerate(piece):
            theirs_at = pl.multiple_of((2 * (z ^ d) + 1 - mine) * share, 8)
            mine_at = pl.multiple_of((2 * (z ^ d) + mine) * share, 8)
            pack_block(picked[pl.ds(theirs_at, share), :], send.at[skip + k])
            keep[k] = picked[pl.ds(mine_at, share), :]


def unpack_block(block, rows):
    scales = unpack_scales(block, rows)
    return jnp.concatenate([unpack_part(block, rows, part, scales) for part in range(2)], axis=0)


def pass_kernel(share, got_ref, keep_ref, out_ref):
    for k in range(got_ref.shape[0]):
        pack_block(keep_ref[k] + unpack_block(got_ref.at[k], share), out_ref.at[k])


def join_kernel(share, got_ref, keep_ref, near_ref, keep_out, *send_out):
    count = got_ref.shape[0]
    for k in range(count):
        total = keep_ref[k] + unpack_block(got_ref.at[k], share)
        total = total + unpack_block(near_ref.at[k], share)
        if k % 2:
            pack_block(total, send_out[0].at[k // 2])
        else:
            keep_out[k // 2] = total


def fold_kernel(share, got_ref, keep_ref, keep_out, *send_out):
    for k in range(got_ref.shape[0]):
        total = keep_ref[k] + unpack_block(got_ref.at[k], share)
        if k % 2:
            pack_block(total, send_out[0].at[k // 2])
        else:
            keep_out[k // 2] = total


def short_join_kernel(share, got_ref, keep_ref, near_ref, *outs):
    for k, out in enumerate(outs):
        total = keep_ref[k] + unpack_block(got_ref.at[k], share)
        if k == 0:
            total = total + unpack_block(near_ref.at[0], share)
        pack_block(total, out.at[0])


def last_kernel(scale, share, chunks, *refs):
    out_ref = refs[-1]
    for c in range(chunks):
        own, got = refs[2 * c : 2 * c + 2]
        value = own[0] + unpack_block(got.at[0], share)
        out_ref[:, c * LANES : (c + 1) * LANES] = value * scale


def short_last_kernel(scale, share, chunks, side_ref, *refs):
    out_ref = refs[-1]
    for c in range(chunks):
        own, near, far = refs[3 * c : 3 * c + 3]
        value = own[0] + unpack_block(side_ref.at[c], share)
        value = value + unpack_block(near.at[0], share) + unpack_block(far.at[0], share)
        out_ref[:, c * LANES : (c + 1) * LANES] = value * scale


def shards(volume, sketch_matrix, brain_voxels):
    taps = kernel_taps()
    ratios = (taps[1] / taps[2], taps[0] / taps[2])
    planes, width_x, width_y, time_local = volume.shape
    cells = width_x * width_y
    slab = planes * cells
    rank = sketch_matrix.shape[1]
    chunks = rank // LANES
    picks = brain_voxels.shape[0]
    n_gz, n_ta = lax.axis_size("gz"), lax.axis_size("ta")
    share = picks // n_ta
    blocks = n_ta // 2
    tile = 6 * width_y
    window = tile + 8
    tiles = slab // tile
    vmem = pl.BlockSpec(memory_space=pltpu.VMEM)
    smem = pl.BlockSpec(memory_space=pltpu.SMEM)
    hbm = pl.BlockSpec(memory_space=pltpu.HBM)
    flat = volume.reshape(slab, time_local)

    def message_shapes(which):
        return [
            jax.ShapeDtypeStruct((2, cells + 8 * parts, LANES), I16)
            for c in which
            for parts in (FAR_PARTS, NEAR_PARTS)
        ]

    def product_scratch(count):
        return [
            pltpu.VMEM((count, cells, time_local), jnp.bfloat16),
            pltpu.VMEM((time_local, rank), jnp.bfloat16),
            pltpu.SemaphoreType.DMA((count + 1,)),
        ]

    def packs_of(which, odd):
        top = planes - 2
        return [
            (c, plane, parts)
            for c in which
            for plane, parts in ((top * odd, FAR_PARTS), (top * (1 - odd), NEAR_PARTS))
        ]

    def edge_plan(odd):
        far, near = (planes - 2) * odd, (planes - 2) * (1 - odd)
        return [far, far + 1, near, near + 1], packs_of([0], odd)

    def middle_plan(odd):
        return list(range(2, planes - 2)), packs_of(range(1, chunks), odd)

    held_shape = jax.ShapeDtypeStruct((planes + 4, cells, LANES), F32)
    picked_shape = jax.ShapeDtypeStruct((picks + window, LANES), F32)
    matrices = (
        pltpu.with_memory_space_constraint(flat, pltpu.HBM),
        pltpu.with_memory_space_constraint(sketch_matrix, pltpu.HBM),
    )
    shapes = message_shapes([0]) + [held_shape] * chunks
    out = pl.pallas_call(
        functools.partial(product_kernel, edge_plan, False, cells, chunks),
        out_shape=shapes,
        in_specs=[hbm, hbm],
        out_specs=[vmem] * len(shapes),
        scratch_shapes=product_scratch(4),
        compiler_params=VMEM,
        cost_estimate=COST,
        name="edge_products",
    )(*matrices)
    messages, prods = list(out[:2]), out[2:]
    prods, brain_voxels = lax.optimization_barrier((prods, brain_voxels))
    first = jnp.sum(
        brain_voxels[None, :] < (jnp.arange(tiles, dtype=jnp.int32) * tile)[:, None],
        axis=1,
        dtype=jnp.int32,
    )
    wide = jnp.broadcast_to(
        jnp.pad(brain_voxels, (0, window), constant_values=-1)[:, None], (picks + window, LANES)
    )

    even_pairs = [(i, i ^ 1) for i in range(n_gz)]
    odd_pairs = []
    for i in range(n_gz):
        for j in range(n_ta):
            partner = (i, j ^ 2) if i in (0, n_gz - 1) else (i + 1 if i % 2 else i - 1, j)
            odd_pairs.append((i * n_ta + j, partner[0] * n_ta + partner[1]))

    pad = pltpu.VMEM((2, width_x * (width_y + 8) + 8, LANES), F32)
    short = blocks == 4

    message_of = lambda count: jax.ShapeDtypeStruct((count, share + 16, LANES), I16)
    kept_of = lambda count: jax.ShapeDtypeStruct((count, share, LANES), F32)

    def sums(kernel, shapes, args, name):
        return pl.pallas_call(
            functools.partial(kernel, share),
            out_shape=shapes,
            in_specs=[vmem] * len(args),
            out_specs=[vmem] * len(shapes),
            compiler_params=VMEM,
            cost_estimate=COST,
            name=name,
        )(*args)

    def across(value, mask):
        return lax.ppermute(value, "ta", [(i, i ^ mask) for i in range(n_ta)])

    results, carried = [], []
    for c in range(chunks):
        near = lax.ppermute(messages[2 * c + 1], "gz", even_pairs)
        far = lax.ppermute(messages[2 * c], ("gz", "ta"), odd_pairs)
        if c == 0:
            shapes = [picked_shape] + message_shapes(range(1, chunks)) + [held_shape] * chunks
            out = pl.pallas_call(
                functools.partial(
                    middle_inner_kernel, ratios, (width_x, width_y), planes, tile,
                    middle_plan, chunks,
                ),
                out_shape=shapes,
                in_specs=[hbm, hbm, vmem, vmem, smem] + [vmem] * chunks,
                out_specs=[vmem] * len(shapes),
                input_output_aliases={5 + i: len(shapes) - chunks + i for i in range(chunks)},
                scratch_shapes=[pad] + product_scratch(planes - 4),
                compiler_params=VMEM,
                cost_estimate=COST,
                name="middle_and_inner_rows",
            )(*matrices, near, wide, first, *prods)
            picked, prods = out[0], list(out[-chunks:])
            messages += out[1:-chunks]
            held = prods[0]
        else:
            held, rows = lax.optimization_barrier((prods[c], rows))
            held, picked = pl.pallas_call(
                functools.partial(later_inner_kernel, ratios, (width_x, width_y), planes, tile),
                out_shape=[held_shape, picked_shape],
                in_specs=[vmem, vmem, vmem, smem],
                out_specs=[vmem] * 2,
                input_output_aliases={0: 0},
                scratch_shapes=[pad],
                compiler_params=VMEM,
                cost_estimate=COST,
                name="inner_rows",
            )(held, near, wide, first)
        if short:
            pieces = ((3,), (2,), (1,), (0,)) if c else ((3,), (2, 1), (0,))
        else:
            pieces = (range(1, blocks, 2), range(0, blocks, 2))
        counts = [len(piece) for piece in pieces]
        ends = carried if c == chunks - 1 else []
        sent = [message_of(count) for count in counts[:-1]] + [message_of(counts[-1] + len(ends))]
        rows = pl.pallas_call(
            functools.partial(
                outer_kernel, ratios, (width_x, width_y), planes, tile, share, pieces, len(ends)
            ),
            out_shape=[held_shape, picked_shape] + sent + [kept_of(count) for count in counts],
            in_specs=[vmem, vmem, vmem, vmem, smem] + [vmem] * len(ends),
            out_specs=[vmem] * (2 + 2 * len(pieces)),
            input_output_aliases={0: 0, 2: 1},
            scratch_shapes=[pad],
            compiler_params=VMEM,
            cost_estimate=COST,
            name="outer_rows",
        )(held, far, picked, wide, first, *ends)[2:]
        sent, kept = rows[: len(pieces)], rows[len(pieces) :]
        one = message_of(1)
        if short:
            side = [across(value, 1) for value in sent[:-1]]
            (out,) = sums(pass_kernel, [one], (side[0], kept[0]), "pass_sums")
            near_got = across(out, 2)
            shapes = [one] * counts[1]
            out = sums(short_join_kernel, shapes, (side[1], kept[1], near_got), "join_sums")
            far_got = across(out[0], 4)
            if len(out) == 1:
                out = [out[0]] + list(sums(pass_kernel, [one], (side[2], kept[2]), "pass_sums"))
            results += [kept[-1], across(out[1], 2), far_got]
            carried.append(sent[-1])
            if c == chunks - 1:
                results = [across(sent[-1], 1)] + results
        else:
            side = [across(value, 1) for value in sent]
            (out,) = sums(pass_kernel, [message_of(counts[0])], (side[0], kept[0]), "pass_sums")
            near_got = across(out, 2)
            count, mask = counts[1], 4
            shapes = [kept_of(count // 2), message_of(count // 2)]
            keep, out = sums(join_kernel, shapes, (side[1], kept[1], near_got), "join_sums")
            while count > 2:
                count //= 2
                shapes = [kept_of(count // 2), message_of(count // 2)]
                keep, out = sums(fold_kernel, shapes, (across(out, mask), keep), "fold_sums")
                mask *= 2
            results += [keep, across(out, mask)]

    return pl.pallas_call(
        functools.partial(
            short_last_kernel if short else last_kernel, taps[2] ** 3, share, chunks
        ),
        out_shape=jax.ShapeDtypeStruct((share, rank), F32),
        in_specs=[vmem] * len(results),
        out_specs=vmem,
        compiler_params=VMEM,
        name="last_sums",
    )(*results)


def solution(mesh):
    in_specs = (P("gz", None, None, "ta"), P("ta", None), P("gz"))
    out_specs = P(("gz", "ta"), None)
    return jax.shard_map(shards, mesh=mesh, in_specs=in_specs, out_specs=out_specs, check_vma=False)
```

```python
import functools
import math

import jax
import jax.numpy as jnp
from jax import lax
from jax.experimental import pallas as pl
from jax.experimental.pallas import tpu as pltpu
from jax.sharding import PartitionSpec as P

LANES = 128
LEVELS = 32766.0
STEPS = 128.0
FAR_PARTS, NEAR_PARTS = 4, 2
VMEM = pltpu.CompilerParams(vmem_limit_bytes=24 * 1024 * 1024)
COST = pl.CostEstimate(flops=0, bytes_accessed=0, transcendentals=0)
F32 = jnp.float32
I16 = jnp.int16


def kernel_taps():
    sigma = 3.0 / (2.0 * math.sqrt(2.0 * math.log(2.0)))
    raw_taps = [math.exp(-0.5 * (shift_k - 2) ** 2 / sigma**2) for shift_k in range(5)]
    summed = sum(raw_taps)
    return [value_k / summed for value_k in raw_taps]


def pack_block(values, out, parts=2):
    rows, cols = values.shape
    size = rows // parts
    codes = []
    for part in range(parts):
        v = values[part * size : (part + 1) * size].reshape(size // 8, 8, cols)
        top = jnp.maximum(jnp.max(jnp.abs(v), axis=0), 1e-30)
        code = jnp.ceil(jnp.log2(top) * STEPS) + 1.0
        inverse = jnp.exp2(code * (-1.0 / STEPS)) * LEVELS
        q = jnp.round(v * inverse[None]).astype(jnp.int32)
        codes.append(code.astype(jnp.int32))
        out[part * size : (part + 1) * size, :] = q.reshape(size, cols).astype(I16)
    out[rows : rows + 8 * parts, :] = jnp.concatenate(codes, axis=0).astype(I16)


def unpack_scales(block, rows, parts=2):
    codes = block[rows : rows + 8 * parts, :].astype(jnp.int32).astype(F32)
    return jnp.exp2(codes * (1.0 / STEPS)) * (1.0 / LEVELS)


def unpack_part(block, rows, part, scales, parts=2):
    size = rows // parts
    q = block[part * size : (part + 1) * size, :].astype(jnp.int32).astype(F32)
    q = q.reshape(size // 8, 8, q.shape[-1]) * scales[part * 8 : part * 8 + 8][None]
    return q.reshape(size, q.shape[-1])


def pack_planes(msgs, prods, packs):
    for msg, (c, plane, parts) in zip(msgs, packs):
        for i in range(2):
            pack_block(prods[c][plane + 2 + i], msg.at[i], parts)


def multiply_planes(source, weights, prods, slots, first, cells):
    for i, slot in enumerate(slots):
        rows = pl.ds(pl.multiple_of((first + i) * cells, cells), cells)
        product = jnp.dot(source[rows, :], weights[...], preferred_element_type=F32)
        for c, prod in enumerate(prods):
            prod[slot] = product[:, c * LANES : (c + 1) * LANES]


def far_kernel(
    planes, cells, chunks, packs_of, v_hbm, w_hbm, bv_hbm, msg_ref, bv_ref, wide_ref, w_ref, *refs
):
    prods, buf, sem = refs[:chunks], refs[chunks], refs[chunks + 1]
    odd = lax.axis_index("gz") % 2
    far = (planes - 2) * odd
    load_bv = pltpu.make_async_copy(bv_hbm, bv_ref, sem.at[0])
    load_bv.start()
    load_w = pltpu.make_async_copy(w_hbm, w_ref, sem.at[1])
    load_w.start()
    rows = pl.ds(pl.multiple_of(far * cells, cells), 2 * cells)
    load_v = pltpu.make_async_copy(v_hbm.at[rows, :], buf, sem.at[2])
    load_v.start()
    load_bv.wait()
    rows, lanes = bv_ref.shape
    for k in range(rows):
        spread = jnp.broadcast_to(bv_ref[k : k + 1, :], (lanes, lanes))
        wide_ref[k * lanes : (k + 1) * lanes, :] = spread.T
    tail = wide_ref.shape[0] - rows * lanes
    wide_ref[rows * lanes :, :] = jnp.full((tail, lanes), -1, jnp.int32)
    load_w.wait()
    load_v.wait()
    multiply_planes(buf, w_ref, prods, (far + 2, far + 3), 0, cells)
    pack_planes((msg_ref,), prods, packs_of([0], odd)[:1])


def near_kernel(planes, cells, chunks, packs_of, v_ref, w_ref, *refs):
    msg, prods = refs[chunks], refs[chunks + 1 :]
    odd = lax.axis_index("gz") % 2
    near = (planes - 2) * (1 - odd)
    multiply_planes(v_ref, w_ref, prods, (near + 2, near + 3), near, cells)
    pack_planes((msg,), prods, packs_of([0], odd)[1:])


def middle_kernel(planes, cells, chunks, packs_of, v_ref, w_ref, *refs):
    msgs, prods = refs[chunks:-chunks], refs[-chunks:]
    multiply_planes(v_ref, w_ref, prods, range(4, planes), 2, cells)
    pack_planes(msgs, prods, packs_of(range(1, chunks), lax.axis_index("gz") % 2))


def unpack_planes(ref, prod, slot, cells, parts, factor):
    size = cells // parts
    for i in range(2):
        block = ref.at[i]
        scales = unpack_scales(block, cells, parts) * factor
        for part in range(parts):
            prod[slot + i, part * size : (part + 1) * size, :] = unpack_part(
                block, cells, part, scales, parts
            )


def smooth_and_pick(ratios, shape, tile, prod, bv_ref, first_ref, pad, first_plane, count, write):
    width_x, width_y = shape
    window = tile + 8
    r1, r2 = ratios
    stride = width_y + 8
    for side in range(2):
        for x in range(width_x + 1):
            pad[side, x * stride : x * stride + 8, :] = jnp.zeros((8, LANES), F32)
    per_tile = tile // width_y
    tiles = width_x // per_tile
    lane = lax.broadcasted_iota(jnp.int32, (window, LANES), 1)

    def blur(at):
        return at[2] + r1 * (at[1] + at[3]) + r2 * (at[0] + at[4])

    for i in range(count):
        side = i % 2
        p = first_plane + i

        def row(x):
            rows = slice(x * width_y, (x + 1) * width_y)
            return blur([prod[p + k, rows, :] for k in range(5)])

        zero = jnp.zeros((width_y, LANES), F32)
        win = [zero, zero, row(0), row(1)]
        for x in range(width_x):
            win.append(row(x + 2) if x + 2 < width_x else zero)
            pad[side, 8 + x * stride : 8 + x * stride + width_y, :] = blur(win)
            win = win[1:]
        found = []
        for t in range(tiles):
            rows = []
            for x in range(t * per_tile, (t + 1) * per_tile):
                base = 6 + x * stride
                rows.append(blur([pad[side, base + k : base + k + width_y, :] for k in range(5)]))
            value = jnp.concatenate(rows, axis=0)
            high = value.astype(jnp.bfloat16)
            low = (value - high.astype(F32)).astype(jnp.bfloat16)
            number = p * tiles + t
            start = pl.multiple_of((first_ref[number] // 8) * 8, 8)
            voxel = bv_ref[pl.ds(start, window), :]
            hits = []
            for left in range(0, tile, LANES):
                right = min(tile - left, LANES)
                hit = jnp.where(voxel == lane + (left + number * tile), 1.0, 0.0)
                hits.append(hit[:, :right].astype(jnp.bfloat16))
            choose = jnp.concatenate(hits, axis=1)
            both = jnp.concatenate([high, low], axis=1)
            out = jnp.dot(choose, both, preferred_element_type=F32)
            found.append((start, out[:, :LANES] + out[:, LANES:]))
        for start, out in found:
            write(start, out)


def inner_kernel(ratios, shape, planes, tile, near_ref, bv_ref, first_ref, prod, picked, pad):
    odd = lax.axis_index("gz") % 2
    unpack_planes(near_ref, prod, (planes + 2) * (1 - odd), shape[0] * shape[1], NEAR_PARTS, 1.0)
    picked[...] = jnp.zeros_like(picked)

    def write(start, out):
        rest = out.shape[0] - 8
        picked[pl.ds(start, 8), :] += out[:8]
        picked[pl.ds(pl.multiple_of(start + 8, 8), rest), :] = out[8:]

    smooth_and_pick(
        ratios, shape, tile, prod, bv_ref, first_ref, pad, 2 * (1 - odd), planes - 2, write
    )


def inner_rows_kernel(ratios, shape, planes, tile, _, near_ref, bv_ref, first_ref, *refs):
    inner_kernel(ratios, shape, planes, tile, near_ref, bv_ref, first_ref, *refs)


def outer_kernel(
    ratios, shape, planes, tile, share, pieces, carries, *refs
):
    _, far_ref, _, bv_ref, first_ref = refs[:5]
    carried, refs = refs[5 : 5 + carries], refs[5 + carries :]
    prod, picked, refs, pad = refs[0], refs[1], refs[2:-1], refs[-1]
    sends, keeps = refs[: len(pieces)], refs[len(pieces) :]
    g, last = lax.axis_index("gz"), lax.axis_size("gz") - 1
    odd = g % 2
    inside = jnp.where((g == 0) | (g == last), 0.0, 1.0)
    unpack_planes(far_ref, prod, (planes + 2) * odd, shape[0] * shape[1], FAR_PARTS, inside)

    def write(start, out):
        picked[pl.ds(start, out.shape[0]), :] += out

    smooth_and_pick(
        ratios, shape, tile, prod, bv_ref, first_ref, pad, (planes - 2) * odd, 2, write
    )
    mine = lax.axis_index("ta") % 2
    z = lax.axis_index("ta") // 2
    for send, keep, piece in zip(sends, keeps, pieces):
        skip = send.shape[0] - len(piece)
        for k in range(skip):
            send[k] = carried[k][0]
        for k, d in enumerate(piece):
            theirs_at = pl.multiple_of((2 * (z ^ d) + 1 - mine) * share, 8)
            mine_at = pl.multiple_of((2 * (z ^ d) + mine) * share, 8)
            parts = (send.shape[1] - share) // 8
            pack_block(picked[pl.ds(theirs_at, share), :], send.at[skip + k], parts)
            keep[k] = picked[pl.ds(mine_at, share), :]


def unpack_block(block, rows):
    parts = (block.shape[0] - rows) // 8
    scales = unpack_scales(block, rows, parts)
    pieces = [unpack_part(block, rows, part, scales, parts) for part in range(parts)]
    return jnp.concatenate(pieces, axis=0)


def pass_kernel(share, got_ref, keep_ref, out_ref):
    parts = (out_ref.shape[1] - share) // 8
    for k in range(got_ref.shape[0]):
        pack_block(keep_ref[k] + unpack_block(got_ref.at[k], share), out_ref.at[k], parts)


def join_kernel(share, got_ref, keep_ref, near_ref, keep_out, *send_out):
    count = got_ref.shape[0]
    for k in range(count):
        total = keep_ref[k] + unpack_block(got_ref.at[k], share)
        total = total + unpack_block(near_ref.at[k], share)
        if k % 2:
            pack_block(total, send_out[0].at[k // 2])
        else:
            keep_out[k // 2] = total


def fold_kernel(share, got_ref, keep_ref, keep_out, *send_out):
    for k in range(got_ref.shape[0]):
        total = keep_ref[k] + unpack_block(got_ref.at[k], share)
        if k % 2:
            pack_block(total, send_out[0].at[k // 2])
        else:
            keep_out[k // 2] = total


def short_join_kernel(share, got_ref, keep_ref, near_ref, *outs):
    for k, out in enumerate(outs):
        total = keep_ref[k] + unpack_block(got_ref.at[k], share)
        if k == 0:
            total = total + unpack_block(near_ref.at[0], share)
        pack_block(total, out.at[0], (out.shape[1] - share) // 8)


def last_kernel(scale, share, chunks, *refs):
    out_ref = refs[-1]
    for c in range(chunks):
        own, got = refs[2 * c : 2 * c + 2]
        value = own[0] + unpack_block(got.at[0], share)
        out_ref[:, c * LANES : (c + 1) * LANES] = value * scale


def short_last_kernel(scale, share, chunks, side_ref, *refs):
    out_ref = refs[-1]
    for c in range(chunks):
        own, near, far = refs[3 * c : 3 * c + 3]
        value = own[0] + unpack_block(side_ref.at[c], share)
        value = value + unpack_block(near.at[0], share) + unpack_block(far.at[0], share)
        out_ref[:, c * LANES : (c + 1) * LANES] = value * scale


def shards(volume, sketch_matrix, brain_voxels):
    taps = kernel_taps()
    ratios = (taps[1] / taps[2], taps[0] / taps[2])
    planes, width_x, width_y, time_local = volume.shape
    cells = width_x * width_y
    slab = planes * cells
    rank = sketch_matrix.shape[1]
    chunks = rank // LANES
    picks = brain_voxels.shape[0]
    n_gz, n_ta = lax.axis_size("gz"), lax.axis_size("ta")
    share = picks // n_ta
    blocks = n_ta // 2
    tile = 6 * width_y
    window = tile + 8
    tiles = slab // tile
    vmem = pl.BlockSpec(memory_space=pltpu.VMEM)
    smem = pl.BlockSpec(memory_space=pltpu.SMEM)
    hbm = pl.BlockSpec(memory_space=pltpu.HBM)
    flat = volume.reshape(slab, time_local)

    def message_shapes(which):
        return [
            jax.ShapeDtypeStruct((2, cells + 8 * parts, LANES), I16)
            for c in which
            for parts in (FAR_PARTS, NEAR_PARTS)
        ]

    def packs_of(which, odd):
        top = planes - 2
        return [
            (c, plane, parts)
            for c in which
            for plane, parts in ((top * odd, FAR_PARTS), (top * (1 - odd), NEAR_PARTS))
        ]

    held_shape = jax.ShapeDtypeStruct((planes + 4, cells, LANES), F32)
    picked_shape = jax.ShapeDtypeStruct((picks + window, LANES), F32)
    indices = brain_voxels.reshape(picks // LANES, LANES)
    shapes = message_shapes([0])[:1] + [
        jax.ShapeDtypeStruct(indices.shape, jnp.int32),
        jax.ShapeDtypeStruct((picks + window, LANES), jnp.int32),
        jax.ShapeDtypeStruct((time_local, rank), jnp.bfloat16),
    ]
    shapes += [held_shape] * chunks
    out = pl.pallas_call(
        functools.partial(far_kernel, planes, cells, chunks, packs_of),
        out_shape=shapes,
        in_specs=[hbm, hbm, hbm],
        out_specs=[vmem] * len(shapes),
        scratch_shapes=[
            pltpu.VMEM((2 * cells, time_local), jnp.bfloat16),
            pltpu.SemaphoreType.DMA((3,)),
        ],
        compiler_params=VMEM,
        cost_estimate=COST,
        name="far_products",
    )(*[pltpu.with_memory_space_constraint(x, pltpu.HBM) for x in (flat, sketch_matrix, indices)])
    far_message, indices, wide, weights = out[:4]
    prods = out[4:]

    def more_products(kernel, shapes, prods, name):
        out = pl.pallas_call(
            functools.partial(kernel, planes, cells, chunks, packs_of),
            out_shape=shapes + [held_shape] * chunks,
            in_specs=[vmem] * (2 + chunks),
            out_specs=[vmem] * (len(shapes) + chunks),
            input_output_aliases={2 + i: len(shapes) + i for i in range(chunks)},
            compiler_params=VMEM,
            cost_estimate=COST,
            name=name,
        )(flat, weights, *prods)
        return list(out[:-chunks]), out[-chunks:]

    near_message, prods = more_products(
        near_kernel, message_shapes([0])[1:], prods, "near_products"
    )
    messages, prods = more_products(
        middle_kernel, message_shapes(range(1, chunks)), prods, "middle_products"
    )
    messages = [far_message] + near_message + messages
    first = jnp.sum(
        indices.reshape(1, picks) < (jnp.arange(tiles, dtype=jnp.int32) * tile)[:, None],
        axis=1,
        dtype=jnp.int32,
    )

    even_pairs = [(i, i ^ 1) for i in range(n_gz)]
    odd_pairs = []
    for i in range(n_gz):
        for j in range(n_ta):
            partner = (i, j ^ 2) if i in (0, n_gz - 1) else (i + 1 if i % 2 else i - 1, j)
            odd_pairs.append((i * n_ta + j, partner[0] * n_ta + partner[1]))

    pad = pltpu.VMEM((2, width_x * (width_y + 8) + 8, LANES), F32)
    short = blocks == 4

    message_of = lambda count: jax.ShapeDtypeStruct((count, share + 16, LANES), I16)
    kept_of = lambda count: jax.ShapeDtypeStruct((count, share, LANES), F32)

    def sums(kernel, shapes, args, name):
        return pl.pallas_call(
            functools.partial(kernel, share),
            out_shape=shapes,
            in_specs=[vmem] * len(args),
            out_specs=[vmem] * len(shapes),
            compiler_params=VMEM,
            cost_estimate=COST,
            name=name,
        )(*args)

    def across(value, mask):
        return lax.ppermute(value, "ta", [(i, i ^ mask) for i in range(n_ta)])

    one, urgent = message_of(1), jax.ShapeDtypeStruct((1, share + 32, LANES), I16)

    def finish(near_got, side, kept, before=None):
        shapes = [urgent, one]
        far, near = sums(short_join_kernel, shapes, (side[0], kept[0], near_got), "join_sums")
        if before is not None:
            near, before[-2] = lax.optimization_barrier((near, before[-2]))
        return far, [kept[-1], across(near, 2), across(far, 4)]

    results, carried, waiting = [], [], None
    for c in range(chunks):
        near = lax.ppermute(messages[2 * c + 1], "gz", even_pairs)
        far = lax.ppermute(messages[2 * c], ("gz", "ta"), odd_pairs)
        held = prods[c]
        if c:
            held, rows = lax.optimization_barrier((held, rows))
        held, picked = pl.pallas_call(
            functools.partial(inner_rows_kernel, ratios, (width_x, width_y), planes, tile),
            out_shape=[held_shape, picked_shape],
            in_specs=[vmem, vmem, vmem, smem],
            out_specs=[vmem] * 2,
            input_output_aliases={0: 0},
            scratch_shapes=[pad],
            compiler_params=VMEM,
            cost_estimate=COST,
            name="inner_rows",
        )(held, near, wide, first)
        if waiting:
            picked, waiting[1] = lax.optimization_barrier((picked, waiting[1]))
            out = sums(pass_kernel, [urgent], waiting[:2], "pass_sums")[0]
            picked, out = lax.optimization_barrier((picked, out))
            waiting[:2] = [across(out, 2)]
        if short:
            pieces = ((3,), (2, 1), (0,))
        else:
            pieces = (range(1, blocks, 2), range(0, blocks, 2))
        counts = [len(piece) for piece in pieces]
        ends = carried if c == chunks - 1 else []
        sent = [message_of(count) for count in counts[:-1]] + [message_of(counts[-1] + len(ends))]
        if short and not waiting:
            sent[1] = jax.ShapeDtypeStruct((counts[1], share + 32, LANES), I16)
        rows = pl.pallas_call(
            functools.partial(
                outer_kernel, ratios, (width_x, width_y), planes, tile, share, pieces, len(ends)
            ),
            out_shape=[held_shape, picked_shape] + sent + [kept_of(count) for count in counts],
            in_specs=[vmem, vmem, vmem, vmem, smem] + [vmem] * len(ends),
            out_specs=[vmem] * (2 + 2 * len(pieces)),
            input_output_aliases={0: 0, 2: 1},
            scratch_shapes=[pad],
            compiler_params=VMEM,
            cost_estimate=COST,
            name="outer_rows",
        )(held, far, picked, wide, first, *ends)[2:]
        sent, kept = rows[: len(pieces)], rows[len(pieces) :]
        if short:
            done = None
            if waiting:
                waiting[0], *sent = lax.optimization_barrier((waiting[0], *sent))
                done, result = finish(*waiting)
                results += result
            side = [across(value, 1) for value in sent[:-1]]
            if done is not None:
                kept = list(kept)
                kept[0], done = lax.optimization_barrier((kept[0], done))
            waiting = [side[0], kept[0], side[1:], kept[1:]]
            carried.append(sent[-1])
            if c == chunks - 1:
                (out,) = sums(pass_kernel, [urgent], waiting[:2], "pass_sums")
                near_got = across(out, 2)
                if results:
                    near_got, results[-1] = lax.optimization_barrier((near_got, results[-1]))
                results += finish(near_got, *waiting[2:], results or None)[1]
                results = [across(sent[-1], 1)] + results
        else:
            side = [across(value, 1) for value in sent]
            (out,) = sums(pass_kernel, [message_of(counts[0])], (side[0], kept[0]), "pass_sums")
            near_got = across(out, 2)
            count, mask = counts[1], 4
            shapes = [kept_of(count // 2), message_of(count // 2)]
            keep, out = sums(join_kernel, shapes, (side[1], kept[1], near_got), "join_sums")
            while count > 2:
                count //= 2
                shapes = [kept_of(count // 2), message_of(count // 2)]
                keep, out = sums(fold_kernel, shapes, (across(out, mask), keep), "fold_sums")
                mask *= 2
            results += [keep, across(out, mask)]

    return pl.pallas_call(
        functools.partial(
            short_last_kernel if short else last_kernel, taps[2] ** 3, share, chunks
        ),
        out_shape=jax.ShapeDtypeStruct((share, rank), F32),
        in_specs=[vmem] * len(results),
        out_specs=vmem,
        compiler_params=VMEM,
        name="last_sums",
    )(*results)


def solution(mesh):
    in_specs = (P("gz", None, None, "ta"), P("ta", None), P("gz"))
    out_specs = P(("gz", "ta"), None)
    return jax.shard_map(shards, mesh=mesh, in_specs=in_specs, out_specs=out_specs, check_vma=False)
```

```python
import functools
import math

import jax
import jax.numpy as jnp
from jax import lax
from jax.experimental import pallas as pl
from jax.experimental.pallas import tpu as pltpu
from jax.sharding import PartitionSpec as P

LANES = 128
LEVELS = 32766.0
STEPS = 128.0
FAR_PARTS, NEAR_PARTS = 4, 2
VMEM = pltpu.CompilerParams(vmem_limit_bytes=24 * 1024 * 1024)
COST = pl.CostEstimate(flops=0, bytes_accessed=0, transcendentals=0)
F32 = jnp.float32
I16 = jnp.int16


def kernel_taps():
    sigma = 3.0 / (2.0 * math.sqrt(2.0 * math.log(2.0)))
    raw_taps = [math.exp(-0.5 * (shift_k - 2) ** 2 / sigma**2) for shift_k in range(5)]
    summed = sum(raw_taps)
    return [value_k / summed for value_k in raw_taps]


def pack_block(values, out, parts=2):
    rows, cols = values.shape
    size = rows // parts
    codes = []
    for part in range(parts):
        v = values[part * size : (part + 1) * size].reshape(size // 8, 8, cols)
        top = jnp.maximum(jnp.max(jnp.abs(v), axis=0), 1e-30)
        code = jnp.ceil(jnp.log2(top) * STEPS) + 1.0
        inverse = jnp.exp2(code * (-1.0 / STEPS)) * LEVELS
        q = jnp.round(v * inverse[None]).astype(jnp.int32)
        codes.append(code.astype(jnp.int32))
        out[part * size : (part + 1) * size, :] = q.reshape(size, cols).astype(I16)
    codes = codes * 2 if parts == 1 else codes
    fill = [jnp.zeros_like(codes[0])] * ((out.shape[0] - rows) // 8 - len(codes))
    out[rows:, :] = jnp.concatenate(codes + fill, axis=0).astype(I16)


def unpack_scales(block, rows, parts=2):
    codes = block[rows : rows + 8 * parts, :].astype(jnp.int32).astype(F32)
    return jnp.exp2(codes * (1.0 / STEPS)) * (1.0 / LEVELS)


def unpack_part(block, rows, part, scales, parts=2):
    size = rows // parts
    q = block[part * size : (part + 1) * size, :].astype(jnp.int32).astype(F32)
    q = q.reshape(size // 8, 8, q.shape[-1]) * scales[part * 8 : part * 8 + 8][None]
    return q.reshape(size, q.shape[-1])


def pack_planes(msgs, prods, packs):
    for msg, (c, plane, parts) in zip(msgs, packs):
        for i in range(2):
            pack_block(prods[c][plane + 2 + i], msg.at[i], parts)


def multiply_planes(source, weights, prods, slots, first, cells):
    for i, slot in enumerate(slots):
        rows = pl.ds(pl.multiple_of((first + i) * cells, cells), cells)
        product = jnp.dot(source[rows, :], weights[...], preferred_element_type=F32)
        for c, prod in enumerate(prods):
            prod[slot] = product[:, c * LANES : (c + 1) * LANES]


def far_kernel(
    planes, cells, chunks, packs_of, v_hbm, w_hbm, bv_hbm, msg_ref, bv_ref, wide_ref, w_ref, *refs
):
    prods, buf, sem = refs[:chunks], refs[chunks], refs[chunks + 1]
    odd = lax.axis_index("gz") % 2
    far = (planes - 2) * odd
    load_bv = pltpu.make_async_copy(bv_hbm, bv_ref, sem.at[0])
    load_bv.start()
    load_w = pltpu.make_async_copy(w_hbm, w_ref, sem.at[1])
    load_w.start()
    rows = pl.ds(pl.multiple_of(far * cells, cells), 2 * cells)
    load_v = pltpu.make_async_copy(v_hbm.at[rows, :], buf, sem.at[2])
    load_v.start()
    load_bv.wait()
    rows, lanes = bv_ref.shape
    for k in range(rows):
        spread = jnp.broadcast_to(bv_ref[k : k + 1, :], (lanes, lanes))
        wide_ref[k * lanes : (k + 1) * lanes, :] = spread.T
    tail = wide_ref.shape[0] - rows * lanes
    wide_ref[rows * lanes :, :] = jnp.full((tail, lanes), -1, jnp.int32)
    load_w.wait()
    load_v.wait()
    multiply_planes(buf, w_ref, prods, (far + 2, far + 3), 0, cells)
    pack_planes((msg_ref,), prods, packs_of([0], odd)[:1])


def near_kernel(planes, cells, chunks, packs_of, v_ref, w_ref, *refs):
    msg, prods = refs[chunks], refs[chunks + 1 :]
    odd = lax.axis_index("gz") % 2
    near = (planes - 2) * (1 - odd)
    multiply_planes(v_ref, w_ref, prods, (near + 2, near + 3), near, cells)
    pack_planes((msg,), prods, packs_of([0], odd)[1:])


def middle_kernel(planes, cells, chunks, packs_of, v_ref, w_ref, *refs):
    msgs, prods = refs[chunks:-chunks], refs[-chunks:]
    multiply_planes(v_ref, w_ref, prods, range(4, planes), 2, cells)
    pack_planes(msgs, prods, packs_of(range(1, chunks), lax.axis_index("gz") % 2))


def unpack_planes(ref, prod, slot, cells, parts, factor):
    size = cells // parts
    for i in range(2):
        block = ref.at[i]
        scales = unpack_scales(block, cells, parts) * factor
        for part in range(parts):
            prod[slot + i, part * size : (part + 1) * size, :] = unpack_part(
                block, cells, part, scales, parts
            )


def smooth_and_pick(ratios, shape, tile, prod, bv_ref, first_ref, pad, first_plane, count, write):
    tiles = shape[0] * shape[1] // tile
    picks = bv_ref.shape[0] - tile - 8
    total = first_ref.shape[0]
    most = jnp.int32(0)
    for i in range(count * tiles):
        number = first_plane * tiles + i
        after = jnp.where(number + 1 < total, first_ref[jnp.minimum(number + 1, total - 1)], picks)
        most = jnp.maximum(most, after - (first_ref[number] // 8) * 8)
    short = tile // 4 * 3 + 4
    args = (ratios, shape, tile, prod, bv_ref, first_ref, pad, first_plane, count, write)

    @pl.when(most <= short)
    def _():
        smooth_tiles(short, *args)

    @pl.when(most > short)
    def _():
        smooth_tiles(tile + 8, *args)


def smooth_tiles(
    window, ratios, shape, tile, prod, bv_ref, first_ref, pad, first_plane, count, write
):
    width_x, width_y = shape
    r1, r2 = ratios
    stride = width_y + 8
    for side in range(2):
        for x in range(width_x + 1):
            pad[side, x * stride : x * stride + 8, :] = jnp.zeros((8, LANES), F32)
    per_tile = tile // width_y
    tiles = width_x // per_tile
    lane = lax.broadcasted_iota(jnp.int32, (window, LANES), 1)

    def blur(at):
        return at[2] + r1 * (at[1] + at[3]) + r2 * (at[0] + at[4])

    for i in range(count):
        side = i % 2
        p = first_plane + i

        def row(x):
            rows = slice(x * width_y, (x + 1) * width_y)
            return blur([prod[p + k, rows, :] for k in range(5)])

        zero = jnp.zeros((width_y, LANES), F32)
        win = [zero, zero, row(0), row(1)]
        for x in range(width_x):
            win.append(row(x + 2) if x + 2 < width_x else zero)
            pad[side, 8 + x * stride : 8 + x * stride + width_y, :] = blur(win)
            win = win[1:]
        found = []
        for t in range(tiles):
            rows = []
            for x in range(t * per_tile, (t + 1) * per_tile):
                base = 6 + x * stride
                rows.append(blur([pad[side, base + k : base + k + width_y, :] for k in range(5)]))
            value = jnp.concatenate(rows, axis=0)
            high = value.astype(jnp.bfloat16)
            low = (value - high.astype(F32)).astype(jnp.bfloat16)
            number = p * tiles + t
            start = pl.multiple_of((first_ref[number] // 8) * 8, 8)
            voxel = bv_ref[pl.ds(start, window), :]
            hits = []
            for left in range(0, tile, LANES):
                right = min(tile - left, LANES)
                hit = jnp.where(voxel == lane + (left + number * tile), 1.0, 0.0)
                hits.append(hit[:, :right].astype(jnp.bfloat16))
            choose = jnp.concatenate(hits, axis=1)
            both = jnp.concatenate([high, low], axis=1)
            out = jnp.dot(choose, both, preferred_element_type=F32)
            found.append((start, out[:, :LANES] + out[:, LANES:]))
        for start, out in found:
            write(start, out)


def inner_kernel(ratios, shape, planes, tile, near_ref, bv_ref, first_ref, prod, picked, pad):
    odd = lax.axis_index("gz") % 2
    unpack_planes(near_ref, prod, (planes + 2) * (1 - odd), shape[0] * shape[1], NEAR_PARTS, 1.0)
    picked[...] = jnp.zeros_like(picked)

    def write(start, out):
        rest = out.shape[0] - 8
        picked[pl.ds(start, 8), :] += out[:8]
        picked[pl.ds(pl.multiple_of(start + 8, 8), rest), :] = out[8:]

    smooth_and_pick(
        ratios, shape, tile, prod, bv_ref, first_ref, pad, 2 * (1 - odd), planes - 2, write
    )


def inner_rows_kernel(ratios, shape, planes, tile, _, near_ref, bv_ref, first_ref, *refs):
    inner_kernel(ratios, shape, planes, tile, near_ref, bv_ref, first_ref, *refs)


def outer_kernel(
    ratios, shape, planes, tile, share, pieces, carries, *refs
):
    _, far_ref, _, bv_ref, first_ref = refs[:5]
    carried, refs = refs[5 : 5 + carries], refs[5 + carries :]
    prod, picked, refs, pad = refs[0], refs[1], refs[2:-1], refs[-1]
    sends, keeps = refs[: len(pieces)], refs[len(pieces) :]
    g, last = lax.axis_index("gz"), lax.axis_size("gz") - 1
    odd = g % 2
    inside = jnp.where((g == 0) | (g == last), 0.0, 1.0)
    unpack_planes(far_ref, prod, (planes + 2) * odd, shape[0] * shape[1], FAR_PARTS, inside)

    def write(start, out):
        picked[pl.ds(start, out.shape[0]), :] += out

    smooth_and_pick(
        ratios, shape, tile, prod, bv_ref, first_ref, pad, (planes - 2) * odd, 2, write
    )
    mine = lax.axis_index("ta") % 2
    z = lax.axis_index("ta") // 2
    for send, keep, piece in zip(sends, keeps, pieces):
        skip = send.shape[0] - len(piece)
        for k in range(skip):
            send[k] = carried[k][0]
        for k, d in enumerate(piece):
            theirs_at = pl.multiple_of((2 * (z ^ d) + 1 - mine) * share, 8)
            mine_at = pl.multiple_of((2 * (z ^ d) + mine) * share, 8)
            parts = parts_of(send.shape[1], share)
            pack_block(picked[pl.ds(theirs_at, share), :], send.at[skip + k], parts)
            keep[k] = picked[pl.ds(mine_at, share), :]


def parts_of(total, rows):
    parts = (total - rows) // 8
    return parts if rows // parts % 16 == 0 else 1


def unpack_block(block, rows):
    parts = parts_of(block.shape[0], rows)
    scales = unpack_scales(block, rows, parts)
    pieces = [unpack_part(block, rows, part, scales, parts) for part in range(parts)]
    return jnp.concatenate(pieces, axis=0)


def pass_kernel(share, got_ref, keep_ref, out_ref):
    parts = parts_of(out_ref.shape[1], share)
    for k in range(got_ref.shape[0]):
        pack_block(keep_ref[k] + unpack_block(got_ref.at[k], share), out_ref.at[k], parts)


def join_kernel(share, got_ref, keep_ref, near_ref, keep_out, *send_out):
    count = got_ref.shape[0]
    for k in range(count):
        total = keep_ref[k] + unpack_block(got_ref.at[k], share)
        total = total + unpack_block(near_ref.at[k], share)
        if k % 2:
            pack_block(total, send_out[0].at[k // 2], parts_of(send_out[0].shape[1], share))
        else:
            keep_out[k // 2] = total


def fold_kernel(share, got_ref, keep_ref, keep_out, *send_out):
    for k in range(got_ref.shape[0]):
        total = keep_ref[k] + unpack_block(got_ref.at[k], share)
        if k % 2:
            pack_block(total, send_out[0].at[k // 2], parts_of(send_out[0].shape[1], share))
        else:
            keep_out[k // 2] = total


def short_join_kernel(share, got_ref, keep_ref, near_ref, *outs):
    for k, out in enumerate(outs):
        total = keep_ref[k] + unpack_block(got_ref.at[k], share)
        if k == 0:
            total = total + unpack_block(near_ref.at[0], share)
        pack_block(total, out.at[0], parts_of(out.shape[1], share))


def last_kernel(scale, share, chunks, *refs):
    out_ref = refs[-1]
    for c in range(chunks):
        own, got = refs[2 * c : 2 * c + 2]
        value = own[0] + unpack_block(got.at[0], share)
        out_ref[:, c * LANES : (c + 1) * LANES] = value * scale


def short_last_kernel(scale, share, chunks, side_ref, *refs):
    out_ref = refs[-1]
    for c in range(chunks):
        own, near, far = refs[3 * c : 3 * c + 3]
        value = own[0] + unpack_block(side_ref.at[c], share)
        value = value + unpack_block(near.at[0], share) + unpack_block(far.at[0], share)
        out_ref[:, c * LANES : (c + 1) * LANES] = value * scale


def shards(volume, sketch_matrix, brain_voxels):
    taps = kernel_taps()
    ratios = (taps[1] / taps[2], taps[0] / taps[2])
    planes, width_x, width_y, time_local = volume.shape
    cells = width_x * width_y
    slab = planes * cells
    rank = sketch_matrix.shape[1]
    chunks = rank // LANES
    picks = brain_voxels.shape[0]
    n_gz, n_ta = lax.axis_size("gz"), lax.axis_size("ta")
    share = picks // n_ta
    blocks = n_ta // 2
    tile = 6 * width_y
    window = tile + 8
    tiles = slab // tile
    vmem = pl.BlockSpec(memory_space=pltpu.VMEM)
    smem = pl.BlockSpec(memory_space=pltpu.SMEM)
    hbm = pl.BlockSpec(memory_space=pltpu.HBM)
    flat = volume.reshape(slab, time_local)

    def message_shapes(which):
        return [
            jax.ShapeDtypeStruct((2, cells + 8 * parts, LANES), I16)
            for c in which
            for parts in (FAR_PARTS, NEAR_PARTS)
        ]

    def packs_of(which, odd):
        top = planes - 2
        return [
            (c, plane, parts)
            for c in which
            for plane, parts in ((top * odd, FAR_PARTS), (top * (1 - odd), NEAR_PARTS))
        ]

    held_shape = jax.ShapeDtypeStruct((planes + 4, cells, LANES), F32)
    picked_shape = jax.ShapeDtypeStruct((picks + window, LANES), F32)
    indices = brain_voxels.reshape(picks // LANES, LANES)
    shapes = message_shapes([0])[:1] + [
        jax.ShapeDtypeStruct(indices.shape, jnp.int32),
        jax.ShapeDtypeStruct((picks + window, LANES), jnp.int32),
        jax.ShapeDtypeStruct((time_local, rank), jnp.bfloat16),
    ]
    shapes += [held_shape] * chunks
    out = pl.pallas_call(
        functools.partial(far_kernel, planes, cells, chunks, packs_of),
        out_shape=shapes,
        in_specs=[hbm, hbm, hbm],
        out_specs=[vmem] * len(shapes),
        scratch_shapes=[
            pltpu.VMEM((2 * cells, time_local), jnp.bfloat16),
            pltpu.SemaphoreType.DMA((3,)),
        ],
        compiler_params=VMEM,
        cost_estimate=COST,
        name="far_products",
    )(*[pltpu.with_memory_space_constraint(x, pltpu.HBM) for x in (flat, sketch_matrix, indices)])
    far_message, indices, wide, weights = out[:4]
    prods = out[4:]

    def more_products(kernel, shapes, prods, name):
        out = pl.pallas_call(
            functools.partial(kernel, planes, cells, chunks, packs_of),
            out_shape=shapes + [held_shape] * chunks,
            in_specs=[vmem] * (2 + chunks),
            out_specs=[vmem] * (len(shapes) + chunks),
            input_output_aliases={2 + i: len(shapes) + i for i in range(chunks)},
            compiler_params=VMEM,
            cost_estimate=COST,
            name=name,
        )(flat, weights, *prods)
        return list(out[:-chunks]), out[-chunks:]

    near_message, prods = more_products(
        near_kernel, message_shapes([0])[1:], prods, "near_products"
    )
    messages, prods = more_products(
        middle_kernel, message_shapes(range(1, chunks)), prods, "middle_products"
    )
    messages = [far_message] + near_message + messages
    first = jnp.sum(
        indices.reshape(1, picks) < (jnp.arange(tiles, dtype=jnp.int32) * tile)[:, None],
        axis=1,
        dtype=jnp.int32,
    )

    even_pairs = [(i, i ^ 1) for i in range(n_gz)]
    odd_pairs = []
    for i in range(n_gz):
        for j in range(n_ta):
            partner = (i, j ^ 2) if i in (0, n_gz - 1) else (i + 1 if i % 2 else i - 1, j)
            odd_pairs.append((i * n_ta + j, partner[0] * n_ta + partner[1]))

    pad = pltpu.VMEM((2, width_x * (width_y + 8) + 8, LANES), F32)
    short = blocks == 4

    message_of = lambda count: jax.ShapeDtypeStruct((count, share + 16, LANES), I16)
    kept_of = lambda count: jax.ShapeDtypeStruct((count, share, LANES), F32)

    def sums(kernel, shapes, args, name):
        return pl.pallas_call(
            functools.partial(kernel, share),
            out_shape=shapes,
            in_specs=[vmem] * len(args),
            out_specs=[vmem] * len(shapes),
            compiler_params=VMEM,
            cost_estimate=COST,
            name=name,
        )(*args)

    def across(value, mask):
        return lax.ppermute(value, "ta", [(i, i ^ mask) for i in range(n_ta)])

    one, urgent, most_urgent = [
        jax.ShapeDtypeStruct((1, share + extra, LANES), I16) for extra in (16, 32, 64)
    ]

    def finish(near_got, side, kept, before=None):
        shapes = [urgent if before else most_urgent, one]
        far, near = sums(short_join_kernel, shapes, (side[0], kept[0], near_got), "join_sums")
        if before is not None:
            near, before[-2] = lax.optimization_barrier((near, before[-2]))
        return far, [kept[-1], across(near, 2), across(far, 4)]

    results, carried, waiting = [], [], None
    for c in range(chunks):
        near = lax.ppermute(messages[2 * c + 1], "gz", even_pairs)
        far = lax.ppermute(messages[2 * c], ("gz", "ta"), odd_pairs)
        held = prods[c]
        if c:
            held, rows = lax.optimization_barrier((held, rows))
        held, picked = pl.pallas_call(
            functools.partial(inner_rows_kernel, ratios, (width_x, width_y), planes, tile),
            out_shape=[held_shape, picked_shape],
            in_specs=[vmem, vmem, vmem, smem],
            out_specs=[vmem] * 2,
            input_output_aliases={0: 0},
            scratch_shapes=[pad],
            compiler_params=VMEM,
            cost_estimate=COST,
            name="inner_rows",
        )(held, near, wide, first)
        if waiting:
            picked, waiting[1] = lax.optimization_barrier((picked, waiting[1]))
            out = sums(pass_kernel, [urgent], waiting[:2], "pass_sums")[0]
            picked, out = lax.optimization_barrier((picked, out))
            waiting[:2] = [across(out, 2)]
        if short:
            pieces = ((3,), (2, 1), (0,))
        else:
            pieces = (range(1, blocks, 2), range(0, blocks, 2))
        counts = [len(piece) for piece in pieces]
        ends = carried if c == chunks - 1 else []
        sent = [message_of(count) for count in counts[:-1]] + [message_of(counts[-1] + len(ends))]
        if short and not waiting:
            sent[1] = jax.ShapeDtypeStruct((counts[1], share + 32, LANES), I16)
        rows = pl.pallas_call(
            functools.partial(
                outer_kernel, ratios, (width_x, width_y), planes, tile, share, pieces, len(ends)
            ),
            out_shape=[held_shape, picked_shape] + sent + [kept_of(count) for count in counts],
            in_specs=[vmem, vmem, vmem, vmem, smem] + [vmem] * len(ends),
            out_specs=[vmem] * (2 + 2 * len(pieces)),
            input_output_aliases={0: 0, 2: 1},
            scratch_shapes=[pad],
            compiler_params=VMEM,
            cost_estimate=COST,
            name="outer_rows",
        )(held, far, picked, wide, first, *ends)[2:]
        sent, kept = list(rows[: len(pieces)]), rows[len(pieces) :]
        if short:
            done = None
            if waiting:
                waiting[0], *sent[1:] = lax.optimization_barrier((waiting[0], *sent[1:]))
                done, result = finish(*waiting)
                results += result
            side = [across(value, 1) for value in sent[:-1]]
            if done is not None:
                kept = list(kept)
                kept[0], done = lax.optimization_barrier((kept[0], done))
            waiting = [side[0], kept[0], side[1:], kept[1:]]
            carried.append(sent[-1])
            if c == chunks - 1:
                (out,) = sums(pass_kernel, [urgent], waiting[:2], "pass_sums")
                near_got = across(out, 2)
                if results:
                    near_got, results[-1] = lax.optimization_barrier((near_got, results[-1]))
                results += finish(near_got, *waiting[2:], results or None)[1]
                results = [across(sent[-1], 1)] + results
        else:
            side = [across(value, 1) for value in sent]
            (out,) = sums(pass_kernel, [message_of(counts[0])], (side[0], kept[0]), "pass_sums")
            near_got = across(out, 2)
            count, mask = counts[1], 4
            shapes = [kept_of(count // 2), message_of(count // 2)]
            keep, out = sums(join_kernel, shapes, (side[1], kept[1], near_got), "join_sums")
            while count > 2:
                count //= 2
                shapes = [kept_of(count // 2), message_of(count // 2)]
                keep, out = sums(fold_kernel, shapes, (across(out, mask), keep), "fold_sums")
                mask *= 2
            results += [keep, across(out, mask)]

    return pl.pallas_call(
        functools.partial(
            short_last_kernel if short else last_kernel, taps[2] ** 3, share, chunks
        ),
        out_shape=jax.ShapeDtypeStruct((share, rank), F32),
        in_specs=[vmem] * len(results),
        out_specs=vmem,
        compiler_params=VMEM,
        name="last_sums",
    )(*results)


def solution(mesh):
    in_specs = (P("gz", None, None, "ta"), P("ta", None), P("gz"))
    out_specs = P(("gz", "ta"), None)
    return jax.shard_map(shards, mesh=mesh, in_specs=in_specs, out_specs=out_specs, check_vma=False)
```

```python
import functools
import math

import jax
import jax.numpy as jnp
from jax import lax
from jax.experimental import pallas as pl
from jax.experimental.pallas import tpu as pltpu
from jax.sharding import PartitionSpec as P

LANES = 128
LEVELS = 32766.0
STEPS = 128.0
FAR_PARTS, NEAR_PARTS = 4, 2
VMEM = pltpu.CompilerParams(vmem_limit_bytes=24 * 1024 * 1024)
COST = pl.CostEstimate(flops=0, bytes_accessed=0, transcendentals=0)
F32 = jnp.float32
I16 = jnp.int16


def kernel_taps():
    sigma = 3.0 / (2.0 * math.sqrt(2.0 * math.log(2.0)))
    raw_taps = [math.exp(-0.5 * (shift_k - 2) ** 2 / sigma**2) for shift_k in range(5)]
    summed = sum(raw_taps)
    return [value_k / summed for value_k in raw_taps]


def pack_block(values, out, parts=2):
    rows, cols = values.shape
    size = rows // parts
    codes = []
    for part in range(parts):
        v = values[part * size : (part + 1) * size].reshape(size // 8, 8, cols)
        top = jnp.maximum(jnp.max(jnp.abs(v), axis=0), 1e-30)
        code = jnp.ceil(jnp.log2(top) * STEPS) + 1.0
        inverse = jnp.exp2(code * (-1.0 / STEPS)) * LEVELS
        q = jnp.round(v * inverse[None]).astype(jnp.int32)
        codes.append(code.astype(jnp.int32))
        out[part * size : (part + 1) * size, :] = q.reshape(size, cols).astype(I16)
    codes = codes * 2 if parts == 1 else codes
    fill = [jnp.zeros_like(codes[0])] * ((out.shape[0] - rows) // 8 - len(codes))
    out[rows:, :] = jnp.concatenate(codes + fill, axis=0).astype(I16)


def unpack_scales(block, rows, parts=2):
    codes = block[rows : rows + 8 * parts, :].astype(jnp.int32).astype(F32)
    return jnp.exp2(codes * (1.0 / STEPS)) * (1.0 / LEVELS)


def unpack_part(block, rows, part, scales, parts=2):
    size = rows // parts
    q = block[part * size : (part + 1) * size, :].astype(jnp.int32).astype(F32)
    q = q.reshape(size // 8, 8, q.shape[-1]) * scales[part * 8 : part * 8 + 8][None]
    return q.reshape(size, q.shape[-1])


def pack_planes(msgs, prods, packs):
    for msg, (c, plane, parts) in zip(msgs, packs):
        for i in range(2):
            pack_block(prods[c][plane + 2 + i], msg.at[i], parts)


def multiply_planes(source, weights, prods, slots, first, cells):
    for i, slot in enumerate(slots):
        rows = pl.ds(pl.multiple_of((first + i) * cells, cells), cells)
        product = jnp.dot(source[rows, :], weights[...], preferred_element_type=F32)
        for c, prod in enumerate(prods):
            prod[slot] = product[:, c * LANES : (c + 1) * LANES]


def far_kernel(
    planes, cells, chunks, packs_of, v_hbm, w_hbm, bv_hbm, msg_ref, bv_ref, wide_ref, w_ref, *refs
):
    prods, buf, sem = refs[:chunks], refs[chunks], refs[chunks + 1]
    odd = lax.axis_index("gz") % 2
    far = (planes - 2) * odd
    load_bv = pltpu.make_async_copy(bv_hbm, bv_ref, sem.at[0])
    load_bv.start()
    load_w = pltpu.make_async_copy(w_hbm, w_ref, sem.at[1])
    load_w.start()
    rows = pl.ds(pl.multiple_of(far * cells, cells), 2 * cells)
    load_v = pltpu.make_async_copy(v_hbm.at[rows, :], buf, sem.at[2])
    load_v.start()
    load_bv.wait()
    rows, lanes = bv_ref.shape
    for k in range(rows):
        spread = jnp.broadcast_to(bv_ref[k : k + 1, :], (lanes, lanes))
        wide_ref[k * lanes : (k + 1) * lanes, :] = spread.T
    tail = wide_ref.shape[0] - rows * lanes
    wide_ref[rows * lanes :, :] = jnp.full((tail, lanes), -1, jnp.int32)
    load_w.wait()
    load_v.wait()
    multiply_planes(buf, w_ref, prods, (far + 2, far + 3), 0, cells)
    pack_planes((msg_ref,), prods, packs_of([0], odd)[:1])


def near_kernel(planes, cells, chunks, packs_of, v_ref, w_ref, *refs):
    msg, prods = refs[chunks], refs[chunks + 1 :]
    odd = lax.axis_index("gz") % 2
    near = (planes - 2) * (1 - odd)
    multiply_planes(v_ref, w_ref, prods, (near + 2, near + 3), near, cells)
    pack_planes((msg,), prods, packs_of([0], odd)[1:])


def middle_kernel(planes, cells, chunks, packs_of, v_ref, w_ref, *refs):
    msgs, prods = refs[chunks:-chunks], refs[-chunks:]
    multiply_planes(v_ref, w_ref, prods, range(4, planes), 2, cells)
    pack_planes(msgs, prods, packs_of(range(1, chunks), lax.axis_index("gz") % 2))


def unpack_planes(ref, prod, slot, cells, parts, factor):
    size = cells // parts
    for i in range(2):
        block = ref.at[i]
        scales = unpack_scales(block, cells, parts) * factor
        for part in range(parts):
            prod[slot + i, part * size : (part + 1) * size, :] = unpack_part(
                block, cells, part, scales, parts
            )


def smooth_and_pick(ratios, shape, tile, prod, bv_ref, first_ref, pad, first_plane, count, write):
    tiles = shape[0] * shape[1] // tile
    picks = bv_ref.shape[0] - tile - 8
    total = first_ref.shape[0]
    most = jnp.int32(0)
    for i in range(count * tiles):
        number = first_plane * tiles + i
        after = jnp.where(number + 1 < total, first_ref[jnp.minimum(number + 1, total - 1)], picks)
        most = jnp.maximum(most, after - (first_ref[number] // 8) * 8)
    short = tile // 4 * 3 + 4
    args = (ratios, shape, tile, prod, bv_ref, first_ref, pad, first_plane, count, write)

    @pl.when(most <= short)
    def _():
        smooth_tiles(short, *args)

    @pl.when(most > short)
    def _():
        smooth_tiles(tile + 8, *args)


def smooth_tiles(
    window, ratios, shape, tile, prod, bv_ref, first_ref, pad, first_plane, count, write
):
    width_x, width_y = shape
    r1, r2 = ratios
    stride = width_y + 8
    for side in range(2):
        for x in range(width_x + 1):
            pad[side, x * stride : x * stride + 8, :] = jnp.zeros((8, LANES), F32)
    per_tile = tile // width_y
    tiles = width_x // per_tile
    lane = lax.broadcasted_iota(jnp.int32, (window, LANES), 1)

    def blur(at):
        return at[2] + r1 * (at[1] + at[3]) + r2 * (at[0] + at[4])

    for i in range(count):
        side = i % 2
        p = first_plane + i

        def row(x):
            rows = slice(x * width_y, (x + 1) * width_y)
            return blur([prod[p + k, rows, :] for k in range(5)])

        zero = jnp.zeros((width_y, LANES), F32)
        win = [zero, zero, row(0), row(1)]
        for x in range(width_x):
            win.append(row(x + 2) if x + 2 < width_x else zero)
            pad[side, 8 + x * stride : 8 + x * stride + width_y, :] = blur(win)
            win = win[1:]
        found = []
        for t in range(tiles):
            rows = []
            for x in range(t * per_tile, (t + 1) * per_tile):
                base = 6 + x * stride
                rows.append(blur([pad[side, base + k : base + k + width_y, :] for k in range(5)]))
            value = jnp.concatenate(rows, axis=0)
            high = value.astype(jnp.bfloat16)
            low = (value - high.astype(F32)).astype(jnp.bfloat16)
            number = p * tiles + t
            start = pl.multiple_of((first_ref[number] // 8) * 8, 8)
            voxel = bv_ref[pl.ds(start, window), :]
            hits = []
            for left in range(0, tile, LANES):
                right = min(tile - left, LANES)
                hit = jnp.where(voxel == lane + (left + number * tile), 1.0, 0.0)
                hits.append(hit[:, :right].astype(jnp.bfloat16))
            choose = jnp.concatenate(hits, axis=1)
            both = jnp.concatenate([high, low], axis=1)
            out = jnp.dot(choose, both, preferred_element_type=F32)
            found.append((start, out[:, :LANES] + out[:, LANES:]))
        for start, out in found:
            write(start, out)


def inner_kernel(ratios, shape, planes, tile, near_ref, bv_ref, first_ref, prod, picked, pad):
    odd = lax.axis_index("gz") % 2
    unpack_planes(near_ref, prod, (planes + 2) * (1 - odd), shape[0] * shape[1], NEAR_PARTS, 1.0)
    picked[...] = jnp.zeros_like(picked)

    def write(start, out):
        rest = out.shape[0] - 8
        picked[pl.ds(start, 8), :] += out[:8]
        picked[pl.ds(pl.multiple_of(start + 8, 8), rest), :] = out[8:]

    smooth_and_pick(
        ratios, shape, tile, prod, bv_ref, first_ref, pad, 2 * (1 - odd), planes - 2, write
    )


def inner_rows_kernel(ratios, shape, planes, tile, _, near_ref, bv_ref, first_ref, *refs):
    inner_kernel(ratios, shape, planes, tile, near_ref, bv_ref, first_ref, *refs)


def outer_kernel(
    ratios, shape, planes, tile, share, pieces, carries, *refs
):
    _, far_ref, _, bv_ref, first_ref = refs[:5]
    carried, refs = refs[5 : 5 + carries], refs[5 + carries :]
    prod, picked, refs, pad = refs[0], refs[1], refs[2:-1], refs[-1]
    sends, keeps = refs[: len(pieces)], refs[len(pieces) :]
    g, last = lax.axis_index("gz"), lax.axis_size("gz") - 1
    odd = g % 2
    inside = jnp.where((g == 0) | (g == last), 0.0, 1.0)
    unpack_planes(far_ref, prod, (planes + 2) * odd, shape[0] * shape[1], FAR_PARTS, inside)

    def write(start, out):
        picked[pl.ds(start, out.shape[0]), :] += out

    smooth_and_pick(
        ratios, shape, tile, prod, bv_ref, first_ref, pad, (planes - 2) * odd, 2, write
    )
    mine = lax.axis_index("ta") % 2
    z = lax.axis_index("ta") // 2
    for send, keep, piece in zip(sends, keeps, pieces):
        skip = send.shape[0] - len(piece)
        for k in range(skip):
            send[k] = carried[k][0]
        for k, d in enumerate(piece):
            theirs_at = pl.multiple_of((2 * (z ^ d) + 1 - mine) * share, 8)
            mine_at = pl.multiple_of((2 * (z ^ d) + mine) * share, 8)
            parts = parts_of(send.shape[1], share)
            pack_block(picked[pl.ds(theirs_at, share), :], send.at[skip + k], parts)
            keep[k] = picked[pl.ds(mine_at, share), :]


def parts_of(total, rows):
    parts = (total - rows) // 8
    return parts if rows // parts % 16 == 0 else 1


def unpack_block(block, rows):
    parts = parts_of(block.shape[0], rows)
    scales = unpack_scales(block, rows, parts)
    pieces = [unpack_part(block, rows, part, scales, parts) for part in range(parts)]
    return jnp.concatenate(pieces, axis=0)


def pass_kernel(share, got_ref, keep_ref, out_ref):
    parts = parts_of(out_ref.shape[1], share)
    for k in range(got_ref.shape[0]):
        pack_block(keep_ref[k] + unpack_block(got_ref.at[k], share), out_ref.at[k], parts)


def join_kernel(share, got_ref, keep_ref, near_ref, keep_out, *send_out):
    count = got_ref.shape[0]
    for k in range(count):
        total = keep_ref[k] + unpack_block(got_ref.at[k], share)
        total = total + unpack_block(near_ref.at[k], share)
        if k % 2:
            pack_block(total, send_out[0].at[k // 2], parts_of(send_out[0].shape[1], share))
        else:
            keep_out[k // 2] = total


def fold_kernel(share, got_ref, keep_ref, keep_out, *send_out):
    for k in range(got_ref.shape[0]):
        total = keep_ref[k] + unpack_block(got_ref.at[k], share)
        if k % 2:
            pack_block(total, send_out[0].at[k // 2], parts_of(send_out[0].shape[1], share))
        else:
            keep_out[k // 2] = total


def short_join_kernel(share, got_ref, keep_ref, near_ref, *outs):
    for k, out in enumerate(outs):
        total = keep_ref[k] + unpack_block(got_ref.at[k], share)
        if k == 0:
            total = total + unpack_block(near_ref.at[0], share)
        pack_block(total, out.at[0], parts_of(out.shape[1], share))


def last_kernel(scale, share, chunks, *refs):
    out_ref = refs[-1]
    for c in range(chunks):
        own, got = refs[2 * c : 2 * c + 2]
        value = own[0] + unpack_block(got.at[0], share)
        out_ref[:, c * LANES : (c + 1) * LANES] = value * scale


def column_kernel(scale, share, chunk, side_ref, own, near, far, *refs):
    out_hbm, buf, sem = refs[-3:]
    half = share // 2
    parts = [unpack_block(ref, share) for ref in (side_ref.at[chunk], near.at[0], far.at[0])]
    copies = []
    for k in range(2):
        rows = slice(k * half, (k + 1) * half)
        buf[rows, :] = (own[0, rows, :] + sum(part[rows] for part in parts)) * scale
        place = out_hbm.at[pl.ds(k * half, half), pl.ds(chunk * LANES, LANES)]
        copies.append(pltpu.make_async_copy(buf.at[pl.ds(k * half, half), :], place, sem.at[k]))
        copies[-1].start()
    for copy in copies:
        copy.wait()


def shards(volume, sketch_matrix, brain_voxels):
    taps = kernel_taps()
    ratios = (taps[1] / taps[2], taps[0] / taps[2])
    planes, width_x, width_y, time_local = volume.shape
    cells = width_x * width_y
    slab = planes * cells
    rank = sketch_matrix.shape[1]
    chunks = rank // LANES
    picks = brain_voxels.shape[0]
    n_gz, n_ta = lax.axis_size("gz"), lax.axis_size("ta")
    share = picks // n_ta
    blocks = n_ta // 2
    tile = 6 * width_y
    window = tile + 8
    tiles = slab // tile
    vmem = pl.BlockSpec(memory_space=pltpu.VMEM)
    smem = pl.BlockSpec(memory_space=pltpu.SMEM)
    hbm = pl.BlockSpec(memory_space=pltpu.HBM)
    flat = volume.reshape(slab, time_local)

    def message_shapes(which):
        return [
            jax.ShapeDtypeStruct((2, cells + 8 * parts, LANES), I16)
            for c in which
            for parts in (FAR_PARTS, NEAR_PARTS)
        ]

    def packs_of(which, odd):
        top = planes - 2
        return [
            (c, plane, parts)
            for c in which
            for plane, parts in ((top * odd, FAR_PARTS), (top * (1 - odd), NEAR_PARTS))
        ]

    held_shape = jax.ShapeDtypeStruct((planes + 4, cells, LANES), F32)
    picked_shape = jax.ShapeDtypeStruct((picks + window, LANES), F32)
    indices = brain_voxels.reshape(picks // LANES, LANES)
    shapes = message_shapes([0])[:1] + [
        jax.ShapeDtypeStruct(indices.shape, jnp.int32),
        jax.ShapeDtypeStruct((picks + window, LANES), jnp.int32),
        jax.ShapeDtypeStruct((time_local, rank), jnp.bfloat16),
    ]
    shapes += [held_shape] * chunks
    out = pl.pallas_call(
        functools.partial(far_kernel, planes, cells, chunks, packs_of),
        out_shape=shapes,
        in_specs=[hbm, hbm, hbm],
        out_specs=[vmem] * len(shapes),
        scratch_shapes=[
            pltpu.VMEM((2 * cells, time_local), jnp.bfloat16),
            pltpu.SemaphoreType.DMA((3,)),
        ],
        compiler_params=VMEM,
        cost_estimate=COST,
        name="far_products",
    )(*[pltpu.with_memory_space_constraint(x, pltpu.HBM) for x in (flat, sketch_matrix, indices)])
    far_message, indices, wide, weights = out[:4]
    prods = out[4:]

    def more_products(kernel, shapes, prods, name):
        out = pl.pallas_call(
            functools.partial(kernel, planes, cells, chunks, packs_of),
            out_shape=shapes + [held_shape] * chunks,
            in_specs=[vmem] * (2 + chunks),
            out_specs=[vmem] * (len(shapes) + chunks),
            input_output_aliases={2 + i: len(shapes) + i for i in range(chunks)},
            compiler_params=VMEM,
            cost_estimate=COST,
            name=name,
        )(flat, weights, *prods)
        return list(out[:-chunks]), out[-chunks:]

    near_message, prods = more_products(
        near_kernel, message_shapes([0])[1:], prods, "near_products"
    )
    messages, prods = more_products(
        middle_kernel, message_shapes(range(1, chunks)), prods, "middle_products"
    )
    messages = [far_message] + near_message + messages
    first = jnp.sum(
        indices.reshape(1, picks) < (jnp.arange(tiles, dtype=jnp.int32) * tile)[:, None],
        axis=1,
        dtype=jnp.int32,
    )

    even_pairs = [(i, i ^ 1) for i in range(n_gz)]
    odd_pairs = []
    for i in range(n_gz):
        for j in range(n_ta):
            partner = (i, j ^ 2) if i in (0, n_gz - 1) else (i + 1 if i % 2 else i - 1, j)
            odd_pairs.append((i * n_ta + j, partner[0] * n_ta + partner[1]))

    pad = pltpu.VMEM((2, width_x * (width_y + 8) + 8, LANES), F32)
    short = blocks == 4

    message_of = lambda count: jax.ShapeDtypeStruct((count, share + 16, LANES), I16)
    kept_of = lambda count: jax.ShapeDtypeStruct((count, share, LANES), F32)

    def sums(kernel, shapes, args, name):
        return pl.pallas_call(
            functools.partial(kernel, share),
            out_shape=shapes,
            in_specs=[vmem] * len(args),
            out_specs=[vmem] * len(shapes),
            compiler_params=VMEM,
            cost_estimate=COST,
            name=name,
        )(*args)

    def across(value, mask):
        return lax.ppermute(value, "ta", [(i, i ^ mask) for i in range(n_ta)])

    one, urgent, most_urgent = [
        jax.ShapeDtypeStruct((1, share + extra, LANES), I16) for extra in (16, 32, 48)
    ]

    def finish(near_got, side, kept, before=None):
        shapes = [urgent if before else most_urgent, one]
        far, near = sums(short_join_kernel, shapes, (side[0], kept[0], near_got), "join_sums")
        if before is not None:
            near, before[-2] = lax.optimization_barrier((near, before[-2]))
        return far, [kept[-1], across(near, 2), across(far, 4)]

    results, carried, waiting = [], [], None
    for c in range(chunks):
        near = lax.ppermute(messages[2 * c + 1], "gz", even_pairs)
        far = lax.ppermute(messages[2 * c], ("gz", "ta"), odd_pairs)
        held = prods[c]
        if c:
            held, rows = lax.optimization_barrier((held, rows))
        held, picked = pl.pallas_call(
            functools.partial(inner_rows_kernel, ratios, (width_x, width_y), planes, tile),
            out_shape=[held_shape, picked_shape],
            in_specs=[vmem, vmem, vmem, smem],
            out_specs=[vmem] * 2,
            input_output_aliases={0: 0},
            scratch_shapes=[pad],
            compiler_params=VMEM,
            cost_estimate=COST,
            name="inner_rows",
        )(held, near, wide, first)
        if short:
            pieces = ((3,), (2, 1), (0,))
        else:
            pieces = (range(1, blocks, 2), range(0, blocks, 2))
        counts = [len(piece) for piece in pieces]
        ends = carried if c == chunks - 1 else []
        sent = [message_of(count) for count in counts[:-1]] + [message_of(counts[-1] + len(ends))]
        rows = pl.pallas_call(
            functools.partial(
                outer_kernel, ratios, (width_x, width_y), planes, tile, share, pieces, len(ends)
            ),
            out_shape=[held_shape, picked_shape] + sent + [kept_of(count) for count in counts],
            in_specs=[vmem, vmem, vmem, vmem, smem] + [vmem] * len(ends),
            out_specs=[vmem] * (2 + 2 * len(pieces)),
            input_output_aliases={0: 0, 2: 1},
            scratch_shapes=[pad],
            compiler_params=VMEM,
            cost_estimate=COST,
            name="outer_rows",
        )(held, far, picked, wide, first, *ends)[2:]
        sent, kept = list(rows[: len(pieces)]), rows[len(pieces) :]
        if short:
            done = None
            if waiting:
                waiting[1], *sent = lax.optimization_barrier((waiting[1], *sent))
                (out,) = sums(pass_kernel, [urgent], waiting[:2], "pass_sums")
                out, *sent = lax.optimization_barrier((out, *sent))
                done, result = finish(across(out, 2), *waiting[2:])
                results += result
            side = [across(value, 1) for value in sent[:-1]]
            if done is not None:
                kept = list(kept)
                kept[0], done = lax.optimization_barrier((kept[0], done))
            waiting = [side[0], kept[0], side[1:], kept[1:]]
            carried.append(sent[-1])
            if c == chunks - 1:
                (out,) = sums(pass_kernel, [urgent], waiting[:2], "pass_sums")
                near_got = across(out, 2)
                if results:
                    near_got, results[-1] = lax.optimization_barrier((near_got, results[-1]))
                results += finish(near_got, *waiting[2:], results or None)[1]
                results = [across(sent[-1], 1)] + results
        else:
            side = [across(value, 1) for value in sent]
            (out,) = sums(pass_kernel, [message_of(counts[0])], (side[0], kept[0]), "pass_sums")
            near_got = across(out, 2)
            count, mask = counts[1], 4
            shapes = [kept_of(count // 2), message_of(count // 2)]
            keep, out = sums(join_kernel, shapes, (side[1], kept[1], near_got), "join_sums")
            while count > 2:
                count //= 2
                shapes = [kept_of(count // 2), message_of(count // 2)]
                keep, out = sums(fold_kernel, shapes, (across(out, mask), keep), "fold_sums")
                mask *= 2
            results += [keep, across(out, mask)]

    result = jax.ShapeDtypeStruct((share, rank), F32)
    if short:
        outs = []
        for c in range(chunks):
            args = [results[0]] + results[1 + 3 * c : 4 + 3 * c]
            outs = [
                pl.pallas_call(
                    functools.partial(column_kernel, taps[2] ** 3, share, c),
                    out_shape=result,
                    in_specs=[vmem] * len(args) + [hbm] * len(outs),
                    out_specs=hbm,
                    input_output_aliases={len(args): 0} if outs else {},
                    scratch_shapes=[
                        pltpu.VMEM((share, LANES), F32),
                        pltpu.SemaphoreType.DMA((2,)),
                    ],
                    compiler_params=VMEM,
                    cost_estimate=COST,
                    name="result_columns",
                )(*args, *outs)
            ]
        return outs[0]
    return pl.pallas_call(
        functools.partial(last_kernel, taps[2] ** 3, share, chunks),
        out_shape=result,
        in_specs=[vmem] * len(results),
        out_specs=vmem,
        compiler_params=VMEM,
        name="last_sums",
    )(*results)


def solution(mesh):
    in_specs = (P("gz", None, None, "ta"), P("ta", None), P("gz"))
    out_specs = P(("gz", "ta"), None)
    return jax.shard_map(shards, mesh=mesh, in_specs=in_specs, out_specs=out_specs, check_vma=False)
```

```python
import functools
import math

import jax
import jax.numpy as jnp
from jax import lax
from jax.experimental import pallas as pl
from jax.experimental.pallas import tpu as pltpu
from jax.sharding import PartitionSpec as P

LANES = 128
LEVELS = 32766.0
STEPS = 128.0
FAR_PARTS, NEAR_PARTS = 4, 2
VMEM = pltpu.CompilerParams(vmem_limit_bytes=24 * 1024 * 1024)
COST = pl.CostEstimate(flops=0, bytes_accessed=0, transcendentals=0)
F32 = jnp.float32
I16 = jnp.int16


def kernel_taps():
    sigma = 3.0 / (2.0 * math.sqrt(2.0 * math.log(2.0)))
    raw_taps = [math.exp(-0.5 * (shift_k - 2) ** 2 / sigma**2) for shift_k in range(5)]
    summed = sum(raw_taps)
    return [value_k / summed for value_k in raw_taps]


def pack_block(values, out, parts=2):
    rows, cols = values.shape
    size = rows // parts
    codes = []
    for part in range(parts):
        v = values[part * size : (part + 1) * size].reshape(size // 8, 8, cols)
        top = jnp.maximum(jnp.max(jnp.abs(v), axis=0), 1e-30)
        code = jnp.ceil(jnp.log2(top) * STEPS) + 1.0
        inverse = jnp.exp2(code * (-1.0 / STEPS)) * LEVELS
        q = jnp.round(v * inverse[None]).astype(jnp.int32)
        codes.append(code.astype(jnp.int32))
        out[part * size : (part + 1) * size, :] = q.reshape(size, cols).astype(I16)
    codes = codes * 2 if parts == 1 else codes
    fill = [jnp.zeros_like(codes[0])] * ((out.shape[0] - rows) // 8 - len(codes))
    out[rows:, :] = jnp.concatenate(codes + fill, axis=0).astype(I16)


def unpack_scales(block, rows, parts=2):
    codes = block[rows : rows + 8 * parts, :].astype(jnp.int32).astype(F32)
    return jnp.exp2(codes * (1.0 / STEPS)) * (1.0 / LEVELS)


def unpack_part(block, rows, part, scales, parts=2):
    size = rows // parts
    q = block[part * size : (part + 1) * size, :].astype(jnp.int32).astype(F32)
    q = q.reshape(size // 8, 8, q.shape[-1]) * scales[part * 8 : part * 8 + 8][None]
    return q.reshape(size, q.shape[-1])


def pack_planes(msgs, prods, packs):
    for msg, (c, plane, parts) in zip(msgs, packs):
        for i in range(2):
            pack_block(prods[c][plane + 2 + i], msg.at[i], parts)


def multiply_planes(source, weights, prods, slots, first, cells):
    rows = pl.ds(pl.multiple_of(first * cells, cells), len(slots) * cells)
    product = jnp.dot(source[rows, :], weights[...], preferred_element_type=F32)
    for i, slot in enumerate(slots):
        for c, prod in enumerate(prods):
            prod[slot] = product[i * cells : (i + 1) * cells, c * LANES : (c + 1) * LANES]


def far_kernel(
    planes, cells, chunks, packs_of, v_hbm, w_hbm, bv_hbm, msg_ref, first_ref, wide_ref, w_ref, *refs
):
    prods, (buf, bv_ref, sem) = refs[:chunks], refs[chunks:]
    odd = lax.axis_index("gz") % 2
    far = (planes - 2) * odd
    load_bv = pltpu.make_async_copy(bv_hbm, bv_ref, sem.at[0])
    load_bv.start()
    load_w = pltpu.make_async_copy(w_hbm, w_ref, sem.at[1])
    load_w.start()
    rows = pl.ds(pl.multiple_of(far * cells, cells), 2 * cells)
    load_v = pltpu.make_async_copy(v_hbm.at[rows, :], buf, sem.at[2])
    load_v.start()
    load_bv.wait()
    rows, lanes = bv_ref.shape
    for k in range(rows):
        spread = jnp.broadcast_to(bv_ref[k : k + 1, :], (lanes, lanes))
        wide_ref[k * lanes : (k + 1) * lanes, :] = spread.T
    tiles = first_ref.shape[0]
    for t in range(tiles):
        below = jnp.where(bv_ref[...] < t * (planes * cells // tiles), 1.0, 0.0)
        first_ref[t] = jnp.sum(below).astype(jnp.int32)
    tail = wide_ref.shape[0] - rows * lanes
    wide_ref[rows * lanes :, :] = jnp.full((tail, lanes), -1, jnp.int32)
    load_w.wait()
    load_v.wait()
    multiply_planes(buf, w_ref, prods, (far + 2, far + 3), 0, cells)
    pack_planes((msg_ref,), prods, packs_of([0], odd)[:1])


def near_kernel(planes, cells, chunks, packs_of, v_ref, w_ref, *refs):
    msg, prods = refs[chunks], refs[chunks + 1 :]
    odd = lax.axis_index("gz") % 2
    near = (planes - 2) * (1 - odd)
    multiply_planes(v_ref, w_ref, prods, (near + 2, near + 3), near, cells)
    pack_planes((msg,), prods, packs_of([0], odd)[1:])


def middle_kernel(planes, cells, chunks, packs_of, v_ref, w_ref, *refs):
    msgs, prods = refs[chunks:-chunks], refs[-chunks:]
    multiply_planes(v_ref, w_ref, prods, range(4, planes), 2, cells)
    pack_planes(msgs, prods, packs_of(range(1, chunks), lax.axis_index("gz") % 2))


def unpack_planes(ref, prod, slot, cells, parts, factor):
    size = cells // parts
    for i in range(2):
        block = ref.at[i]
        scales = unpack_scales(block, cells, parts) * factor
        for part in range(parts):
            prod[slot + i, part * size : (part + 1) * size, :] = unpack_part(
                block, cells, part, scales, parts
            )


def smooth_and_pick(ratios, shape, tile, prod, bv_ref, first_ref, pad, first_plane, count, write):
    tiles = shape[0] * shape[1] // tile
    picks = bv_ref.shape[0] - tile - 8
    total = first_ref.shape[0]
    most = jnp.int32(0)
    for i in range(count * tiles):
        number = first_plane * tiles + i
        after = jnp.where(number + 1 < total, first_ref[jnp.minimum(number + 1, total - 1)], picks)
        most = jnp.maximum(most, after - (first_ref[number] // 8) * 8)
    short = tile // 4 * 3 + 4
    args = (ratios, shape, tile, prod, bv_ref, first_ref, pad, first_plane, count, write)

    @pl.when(most <= short)
    def _():
        smooth_tiles(short, *args)

    @pl.when(most > short)
    def _():
        smooth_tiles(tile + 8, *args)


def smooth_tiles(
    window, ratios, shape, tile, prod, bv_ref, first_ref, pad, first_plane, count, write
):
    width_x, width_y = shape
    r1, r2 = ratios
    stride = width_y + 8
    for side in range(2):
        for x in range(width_x + 1):
            pad[side, x * stride : x * stride + 8, :] = jnp.zeros((8, LANES), F32)
    per_tile = tile // width_y
    tiles = width_x // per_tile
    lane = lax.broadcasted_iota(jnp.int32, (window, LANES), 1)

    def blur(at):
        return at[2] + r1 * (at[1] + at[3]) + r2 * (at[0] + at[4])

    for i in range(count):
        side = i % 2
        p = first_plane + i

        def row(x):
            rows = slice(x * width_y, (x + 1) * width_y)
            return blur([prod[p + k, rows, :] for k in range(5)])

        zero = jnp.zeros((width_y, LANES), F32)
        win = [zero, zero, row(0), row(1)]
        for x in range(width_x):
            win.append(row(x + 2) if x + 2 < width_x else zero)
            pad[side, 8 + x * stride : 8 + x * stride + width_y, :] = blur(win)
            win = win[1:]
        found = []
        for t in range(tiles):
            rows = []
            for x in range(t * per_tile, (t + 1) * per_tile):
                base = 6 + x * stride
                rows.append(blur([pad[side, base + k : base + k + width_y, :] for k in range(5)]))
            value = jnp.concatenate(rows, axis=0)
            high = value.astype(jnp.bfloat16)
            low = (value - high.astype(F32)).astype(jnp.bfloat16)
            number = p * tiles + t
            start = pl.multiple_of((first_ref[number] // 8) * 8, 8)
            voxel = bv_ref[pl.ds(start, window), :]
            hits = []
            for left in range(0, tile, LANES):
                right = min(tile - left, LANES)
                hit = jnp.where(voxel == lane + (left + number * tile), 1.0, 0.0)
                hits.append(hit[:, :right].astype(jnp.bfloat16))
            choose = jnp.concatenate(hits, axis=1)
            both = jnp.concatenate([high, low], axis=1)
            out = jnp.dot(choose, both, preferred_element_type=F32)
            found.append((start, out[:, :LANES] + out[:, LANES:]))
        for start, out in found:
            write(start, out)


def inner_kernel(ratios, shape, planes, tile, near_ref, bv_ref, first_ref, prod, picked, pad):
    odd = lax.axis_index("gz") % 2
    unpack_planes(near_ref, prod, (planes + 2) * (1 - odd), shape[0] * shape[1], NEAR_PARTS, 1.0)
    picked[...] = jnp.zeros_like(picked)

    def write(start, out):
        rest = out.shape[0] - 8
        picked[pl.ds(start, 8), :] += out[:8]
        picked[pl.ds(pl.multiple_of(start + 8, 8), rest), :] = out[8:]

    smooth_and_pick(
        ratios, shape, tile, prod, bv_ref, first_ref, pad, 2 * (1 - odd), planes - 2, write
    )


def inner_rows_kernel(ratios, shape, planes, tile, _, near_ref, bv_ref, first_ref, *refs):
    inner_kernel(ratios, shape, planes, tile, near_ref, bv_ref, first_ref, *refs)


def outer_kernel(
    ratios, shape, planes, tile, share, pieces, carries, *refs
):
    _, far_ref, _, bv_ref, first_ref = refs[:5]
    carried, refs = refs[5 : 5 + carries], refs[5 + carries :]
    prod, picked, refs, pad = refs[0], refs[1], refs[2:-1], refs[-1]
    sends, keeps = refs[: len(pieces)], refs[len(pieces) :]
    g, last = lax.axis_index("gz"), lax.axis_size("gz") - 1
    odd = g % 2
    inside = jnp.where((g == 0) | (g == last), 0.0, 1.0)
    unpack_planes(far_ref, prod, (planes + 2) * odd, shape[0] * shape[1], FAR_PARTS, inside)

    def write(start, out):
        picked[pl.ds(start, out.shape[0]), :] += out

    smooth_and_pick(
        ratios, shape, tile, prod, bv_ref, first_ref, pad, (planes - 2) * odd, 2, write
    )
    mine = lax.axis_index("ta") % 2
    z = lax.axis_index("ta") // 2
    for send, keep, piece in zip(sends, keeps, pieces):
        skip = send.shape[0] - len(piece)
        for k in range(skip):
            send[k] = carried[k][0]
        for k, d in enumerate(piece):
            theirs_at = pl.multiple_of((2 * (z ^ d) + 1 - mine) * share, 8)
            mine_at = pl.multiple_of((2 * (z ^ d) + mine) * share, 8)
            parts = parts_of(send.shape[1], share)
            pack_block(picked[pl.ds(theirs_at, share), :], send.at[skip + k], parts)
            keep[k] = picked[pl.ds(mine_at, share), :]


def parts_of(total, rows):
    parts = (total - rows) // 8
    return parts if rows // parts % 16 == 0 else 1


def unpack_block(block, rows):
    parts = parts_of(block.shape[0], rows)
    scales = unpack_scales(block, rows, parts)
    pieces = [unpack_part(block, rows, part, scales, parts) for part in range(parts)]
    return jnp.concatenate(pieces, axis=0)


def pass_kernel(share, got_ref, keep_ref, out_ref):
    parts = parts_of(out_ref.shape[1], share)
    for k in range(got_ref.shape[0]):
        pack_block(keep_ref[k] + unpack_block(got_ref.at[k], share), out_ref.at[k], parts)


def join_kernel(share, got_ref, keep_ref, near_ref, keep_out, *send_out):
    count = got_ref.shape[0]
    for k in range(count):
        total = keep_ref[k] + unpack_block(got_ref.at[k], share)
        total = total + unpack_block(near_ref.at[k], share)
        if k % 2:
            pack_block(total, send_out[0].at[k // 2], parts_of(send_out[0].shape[1], share))
        else:
            keep_out[k // 2] = total


def fold_kernel(share, got_ref, keep_ref, keep_out, *send_out):
    for k in range(got_ref.shape[0]):
        total = keep_ref[k] + unpack_block(got_ref.at[k], share)
        if k % 2:
            pack_block(total, send_out[0].at[k // 2], parts_of(send_out[0].shape[1], share))
        else:
            keep_out[k // 2] = total


def short_join_kernel(share, got_ref, keep_ref, near_ref, *outs):
    for k, out in enumerate(outs):
        total = keep_ref[k] + unpack_block(got_ref.at[k], share)
        if k == 0:
            total = total + unpack_block(near_ref.at[0], share)
        pack_block(total, out.at[0], parts_of(out.shape[1], share))


def last_kernel(scale, share, chunks, *refs):
    out_ref = refs[-1]
    for c in range(chunks):
        own, got = refs[2 * c : 2 * c + 2]
        value = own[0] + unpack_block(got.at[0], share)
        out_ref[:, c * LANES : (c + 1) * LANES] = value * scale


def column_kernel(scale, share, chunk, side_ref, own, near, far, *refs):
    out_hbm, buf, sem = refs[-3:]
    half = share // 2
    parts = [unpack_block(ref, share) for ref in (side_ref.at[chunk], near.at[0], far.at[0])]
    copies = []
    for k in range(2):
        rows = slice(k * half, (k + 1) * half)
        buf[rows, :] = (own[0, rows, :] + sum(part[rows] for part in parts)) * scale
        place = out_hbm.at[pl.ds(k * half, half), pl.ds(chunk * LANES, LANES)]
        copies.append(pltpu.make_async_copy(buf.at[pl.ds(k * half, half), :], place, sem.at[k]))
        copies[-1].start()
    for copy in copies:
        copy.wait()


def shards(volume, sketch_matrix, brain_voxels):
    taps = kernel_taps()
    ratios = (taps[1] / taps[2], taps[0] / taps[2])
    planes, width_x, width_y, time_local = volume.shape
    cells = width_x * width_y
    slab = planes * cells
    rank = sketch_matrix.shape[1]
    chunks = rank // LANES
    picks = brain_voxels.shape[0]
    n_gz, n_ta = lax.axis_size("gz"), lax.axis_size("ta")
    share = picks // n_ta
    blocks = n_ta // 2
    tile = 6 * width_y
    window = tile + 8
    tiles = slab // tile
    vmem = pl.BlockSpec(memory_space=pltpu.VMEM)
    smem = pl.BlockSpec(memory_space=pltpu.SMEM)
    hbm = pl.BlockSpec(memory_space=pltpu.HBM)
    flat = volume.reshape(slab, time_local)

    def message_shapes(which):
        return [
            jax.ShapeDtypeStruct((2, cells + 8 * parts, LANES), I16)
            for c in which
            for parts in (FAR_PARTS, NEAR_PARTS)
        ]

    def packs_of(which, odd):
        top = planes - 2
        return [
            (c, plane, parts)
            for c in which
            for plane, parts in ((top * odd, FAR_PARTS), (top * (1 - odd), NEAR_PARTS))
        ]

    held_shape = jax.ShapeDtypeStruct((planes + 4, cells, LANES), F32)
    picked_shape = jax.ShapeDtypeStruct((picks + window, LANES), F32)
    indices = brain_voxels.reshape(picks // LANES, LANES)
    shapes = message_shapes([0])[:1] + [
        jax.ShapeDtypeStruct((tiles,), jnp.int32),
        jax.ShapeDtypeStruct((picks + window, LANES), jnp.int32),
        jax.ShapeDtypeStruct((time_local, rank), jnp.bfloat16),
    ]
    shapes += [held_shape] * chunks
    out = pl.pallas_call(
        functools.partial(far_kernel, planes, cells, chunks, packs_of),
        out_shape=shapes,
        in_specs=[hbm, hbm, hbm],
        out_specs=[vmem, smem] + [vmem] * (len(shapes) - 2),
        scratch_shapes=[
            pltpu.VMEM((2 * cells, time_local), jnp.bfloat16),
            pltpu.VMEM(indices.shape, jnp.int32),
            pltpu.SemaphoreType.DMA((3,)),
        ],
        compiler_params=VMEM,
        cost_estimate=COST,
        name="far_products",
    )(*[pltpu.with_memory_space_constraint(x, pltpu.HBM) for x in (flat, sketch_matrix, indices)])
    far_message, first, wide, weights = out[:4]
    prods = out[4:]

    def more_products(kernel, shapes, prods, name):
        out = pl.pallas_call(
            functools.partial(kernel, planes, cells, chunks, packs_of),
            out_shape=shapes + [held_shape] * chunks,
            in_specs=[vmem] * (2 + chunks),
            out_specs=[vmem] * (len(shapes) + chunks),
            input_output_aliases={2 + i: len(shapes) + i for i in range(chunks)},
            compiler_params=VMEM,
            cost_estimate=COST,
            name=name,
        )(flat, weights, *prods)
        return list(out[:-chunks]), out[-chunks:]

    near_message, prods = more_products(
        near_kernel, message_shapes([0])[1:], prods, "near_products"
    )
    messages, prods = more_products(
        middle_kernel, message_shapes(range(1, chunks)), prods, "middle_products"
    )
    messages = [far_message] + near_message + messages

    even_pairs = [(i, i ^ 1) for i in range(n_gz)]
    odd_pairs = []
    for i in range(n_gz):
        for j in range(n_ta):
            partner = (i, j ^ 2) if i in (0, n_gz - 1) else (i + 1 if i % 2 else i - 1, j)
            odd_pairs.append((i * n_ta + j, partner[0] * n_ta + partner[1]))

    pad = pltpu.VMEM((2, width_x * (width_y + 8) + 8, LANES), F32)
    short = blocks == 4

    message_of = lambda count: jax.ShapeDtypeStruct((count, share + 16, LANES), I16)
    kept_of = lambda count: jax.ShapeDtypeStruct((count, share, LANES), F32)

    def sums(kernel, shapes, args, name):
        return pl.pallas_call(
            functools.partial(kernel, share),
            out_shape=shapes,
            in_specs=[vmem] * len(args),
            out_specs=[vmem] * len(shapes),
            compiler_params=VMEM,
            cost_estimate=COST,
            name=name,
        )(*args)

    def across(value, mask):
        return lax.ppermute(value, "ta", [(i, i ^ mask) for i in range(n_ta)])

    one, urgent, most_urgent = [
        jax.ShapeDtypeStruct((1, share + extra, LANES), I16) for extra in (16, 32, 48)
    ]

    def finish(near_got, side, kept, before=None):
        shapes = [urgent if before else most_urgent, one]
        far, near = sums(short_join_kernel, shapes, (side[0], kept[0], near_got), "join_sums")
        if before is not None:
            near, before[-2] = lax.optimization_barrier((near, before[-2]))
        return far, [kept[-1], across(near, 2), across(far, 4)]

    results, carried, waiting = [], [], None
    for c in range(chunks):
        near = lax.ppermute(messages[2 * c + 1], "gz", even_pairs)
        far = lax.ppermute(messages[2 * c], ("gz", "ta"), odd_pairs)
        held = prods[c]
        if c:
            held, rows = lax.optimization_barrier((held, rows))
        held, picked = pl.pallas_call(
            functools.partial(inner_rows_kernel, ratios, (width_x, width_y), planes, tile),
            out_shape=[held_shape, picked_shape],
            in_specs=[vmem, vmem, vmem, smem],
            out_specs=[vmem] * 2,
            input_output_aliases={0: 0},
            scratch_shapes=[pad],
            compiler_params=VMEM,
            cost_estimate=COST,
            name="inner_rows",
        )(held, near, wide, first)
        if short:
            pieces = ((3,), (2, 1), (0,))
        else:
            pieces = (range(1, blocks, 2), range(0, blocks, 2))
        counts = [len(piece) for piece in pieces]
        ends = carried if c == chunks - 1 else []
        sent = [message_of(count) for count in counts[:-1]] + [message_of(counts[-1] + len(ends))]
        rows = pl.pallas_call(
            functools.partial(
                outer_kernel, ratios, (width_x, width_y), planes, tile, share, pieces, len(ends)
            ),
            out_shape=[held_shape, picked_shape] + sent + [kept_of(count) for count in counts],
            in_specs=[vmem, vmem, vmem, vmem, smem] + [vmem] * len(ends),
            out_specs=[vmem] * (2 + 2 * len(pieces)),
            input_output_aliases={0: 0, 2: 1},
            scratch_shapes=[pad],
            compiler_params=VMEM,
            cost_estimate=COST,
            name="outer_rows",
        )(held, far, picked, wide, first, *ends)[2:]
        sent, kept = list(rows[: len(pieces)]), rows[len(pieces) :]
        if short:
            done = None
            if waiting:
                waiting[1], *sent = lax.optimization_barrier((waiting[1], *sent))
                (out,) = sums(pass_kernel, [urgent], waiting[:2], "pass_sums")
                out, *sent = lax.optimization_barrier((out, *sent))
                done, result = finish(across(out, 2), *waiting[2:])
                results += result
            side = [across(value, 1) for value in sent[:-1]]
            if done is not None:
                kept = list(kept)
                kept[0], done = lax.optimization_barrier((kept[0], done))
            waiting = [side[0], kept[0], side[1:], kept[1:]]
            carried.append(sent[-1])
            if c == chunks - 1:
                (out,) = sums(pass_kernel, [urgent], waiting[:2], "pass_sums")
                near_got = across(out, 2)
                if results:
                    near_got, results[-1] = lax.optimization_barrier((near_got, results[-1]))
                results += finish(near_got, *waiting[2:], results or None)[1]
                results = [across(sent[-1], 1)] + results
        else:
            side = [across(value, 1) for value in sent]
            (out,) = sums(pass_kernel, [message_of(counts[0])], (side[0], kept[0]), "pass_sums")
            near_got = across(out, 2)
            count, mask = counts[1], 4
            shapes = [kept_of(count // 2), message_of(count // 2)]
            keep, out = sums(join_kernel, shapes, (side[1], kept[1], near_got), "join_sums")
            while count > 2:
                count //= 2
                shapes = [kept_of(count // 2), message_of(count // 2)]
                keep, out = sums(fold_kernel, shapes, (across(out, mask), keep), "fold_sums")
                mask *= 2
            results += [keep, across(out, mask)]

    result = jax.ShapeDtypeStruct((share, rank), F32)
    if short:
        outs = []
        for c in range(chunks):
            args = [results[0]] + results[1 + 3 * c : 4 + 3 * c]
            outs = [
                pl.pallas_call(
                    functools.partial(column_kernel, taps[2] ** 3, share, c),
                    out_shape=result,
                    in_specs=[vmem] * len(args) + [hbm] * len(outs),
                    out_specs=hbm,
                    input_output_aliases={len(args): 0} if outs else {},
                    scratch_shapes=[
                        pltpu.VMEM((share, LANES), F32),
                        pltpu.SemaphoreType.DMA((2,)),
                    ],
                    compiler_params=VMEM,
                    cost_estimate=COST,
                    name="result_columns",
                )(*args, *outs)
            ]
        return outs[0]
    return pl.pallas_call(
        functools.partial(last_kernel, taps[2] ** 3, share, chunks),
        out_shape=result,
        in_specs=[vmem] * len(results),
        out_specs=vmem,
        compiler_params=VMEM,
        name="last_sums",
    )(*results)


def solution(mesh):
    in_specs = (P("gz", None, None, "ta"), P("ta", None), P("gz"))
    out_specs = P(("gz", "ta"), None)
    return jax.shard_map(shards, mesh=mesh, in_specs=in_specs, out_specs=out_specs, check_vma=False)
```

```python
import functools
import math

import jax
import jax.numpy as jnp
from jax import lax
from jax.experimental import pallas as pl
from jax.experimental.pallas import tpu as pltpu
from jax.sharding import PartitionSpec as P

LANES = 128
LEVELS = 32766.0
STEPS = 128.0
FAR_PARTS, NEAR_PARTS = 4, 2
VMEM = pltpu.CompilerParams(vmem_limit_bytes=24 * 1024 * 1024)
COST = pl.CostEstimate(flops=0, bytes_accessed=0, transcendentals=0)
F32 = jnp.float32
I16 = jnp.int16


def kernel_taps():
    sigma = 3.0 / (2.0 * math.sqrt(2.0 * math.log(2.0)))
    raw_taps = [math.exp(-0.5 * (shift_k - 2) ** 2 / sigma**2) for shift_k in range(5)]
    summed = sum(raw_taps)
    return [value_k / summed for value_k in raw_taps]


def pack_block(values, out, parts=2):
    rows, cols = values.shape
    size = rows // parts
    codes = []
    for part in range(parts):
        v = values[part * size : (part + 1) * size].reshape(size // 8, 8, cols)
        top = jnp.maximum(jnp.max(jnp.abs(v), axis=0), 1e-30)
        code = jnp.ceil(jnp.log2(top) * STEPS) + 1.0
        inverse = jnp.exp2(code * (-1.0 / STEPS)) * LEVELS
        q = jnp.round(v * inverse[None]).astype(jnp.int32)
        codes.append(code.astype(jnp.int32))
        out[part * size : (part + 1) * size, :] = q.reshape(size, cols).astype(I16)
    codes = codes * 2 if parts == 1 else codes
    fill = [jnp.zeros_like(codes[0])] * ((out.shape[0] - rows) // 8 - len(codes))
    out[rows:, :] = jnp.concatenate(codes + fill, axis=0).astype(I16)


def unpack_scales(block, rows, parts=2):
    codes = block[rows : rows + 8 * parts, :].astype(jnp.int32).astype(F32)
    return jnp.exp2(codes * (1.0 / STEPS)) * (1.0 / LEVELS)


def unpack_part(block, rows, part, scales, parts=2):
    size = rows // parts
    q = block[part * size : (part + 1) * size, :].astype(jnp.int32).astype(F32)
    q = q.reshape(size // 8, 8, q.shape[-1]) * scales[part * 8 : part * 8 + 8][None]
    return q.reshape(size, q.shape[-1])


def pack_planes(msgs, prods, packs):
    for msg, (c, plane, parts) in zip(msgs, packs):
        for i in range(2):
            pack_block(prods[c][plane + 2 + i], msg.at[i], parts)


def multiply_planes(source, weights, prods, slots, first, cells):
    rows = pl.ds(pl.multiple_of(first * cells, cells), len(slots) * cells)
    product = jnp.dot(source[rows, :], weights[...], preferred_element_type=F32)
    for i, slot in enumerate(slots):
        for c, prod in enumerate(prods):
            prod[slot] = product[i * cells : (i + 1) * cells, c * LANES : (c + 1) * LANES]


def far_kernel(
    planes, cells, chunks, packs_of, v_hbm, w_hbm, bv_hbm, msg_ref, first_ref, wide_ref, w_ref, *refs
):
    prods, (buf, bv_ref, sem) = refs[:chunks], refs[chunks:]
    odd = lax.axis_index("gz") % 2
    far = (planes - 2) * odd
    load_bv = pltpu.make_async_copy(bv_hbm, bv_ref, sem.at[0])
    load_bv.start()
    load_w = pltpu.make_async_copy(w_hbm, w_ref, sem.at[1])
    load_w.start()
    rows = pl.ds(pl.multiple_of(far * cells, cells), 2 * cells)
    load_v = pltpu.make_async_copy(v_hbm.at[rows, :], buf, sem.at[2])
    load_v.start()
    load_bv.wait()
    rows, lanes = bv_ref.shape
    for k in range(rows):
        spread = jnp.broadcast_to(bv_ref[k : k + 1, :], (lanes, lanes))
        wide_ref[k * lanes : (k + 1) * lanes, :] = spread.T
    tiles = first_ref.shape[0]
    for t in range(tiles):
        below = jnp.where(bv_ref[...] < t * (planes * cells // tiles), 1.0, 0.0)
        first_ref[t] = jnp.sum(below).astype(jnp.int32)
    tail = wide_ref.shape[0] - rows * lanes
    wide_ref[rows * lanes :, :] = jnp.full((tail, lanes), -1, jnp.int32)
    load_w.wait()
    load_v.wait()
    multiply_planes(buf, w_ref, prods, (far + 2, far + 3), 0, cells)
    pack_planes((msg_ref,), prods, packs_of([0], odd)[:1])


def near_kernel(planes, cells, chunks, packs_of, v_ref, w_ref, *refs):
    msg, prods = refs[chunks], refs[chunks + 1 :]
    odd = lax.axis_index("gz") % 2
    near = (planes - 2) * (1 - odd)
    multiply_planes(v_ref, w_ref, prods, (near + 2, near + 3), near, cells)
    pack_planes((msg,), prods, packs_of([0], odd)[1:])


def middle_kernel(planes, cells, chunks, packs_of, v_ref, w_ref, *refs):
    msgs, prods = refs[chunks:-chunks], refs[-chunks:]
    multiply_planes(v_ref, w_ref, prods, range(4, planes), 2, cells)
    pack_planes(msgs, prods, packs_of(range(1, chunks), lax.axis_index("gz") % 2))


def unpack_planes(ref, prod, slot, cells, parts, factor):
    size = cells // parts
    for i in range(2):
        block = ref.at[i]
        scales = unpack_scales(block, cells, parts) * factor
        for part in range(parts):
            prod[slot + i, part * size : (part + 1) * size, :] = unpack_part(
                block, cells, part, scales, parts
            )


def smooth_and_pick(ratios, shape, tile, prod, bv_ref, first_ref, pad, first_plane, count, write):
    tiles = shape[0] * shape[1] // tile
    picks = bv_ref.shape[0] - tile - 8
    total = first_ref.shape[0]
    most = jnp.int32(0)
    for i in range(count * tiles):
        number = first_plane * tiles + i
        after = jnp.where(number + 1 < total, first_ref[jnp.minimum(number + 1, total - 1)], picks)
        most = jnp.maximum(most, after - (first_ref[number] // 8) * 8)
    short = tile // 4 * 3 + 4
    args = (ratios, shape, tile, prod, bv_ref, first_ref, pad, first_plane, count, write)

    @pl.when(most <= short)
    def _():
        smooth_tiles(short, *args)

    @pl.when(most > short)
    def _():
        smooth_tiles(tile + 8, *args)


def smooth_tiles(
    window, ratios, shape, tile, prod, bv_ref, first_ref, pad, first_plane, count, write
):
    width_x, width_y = shape
    r1, r2 = ratios
    stride = width_y + 8
    for side in range(2):
        for x in range(width_x + 1):
            pad[side, x * stride : x * stride + 8, :] = jnp.zeros((8, LANES), F32)
    per_tile = tile // width_y
    tiles = width_x // per_tile
    lane = lax.broadcasted_iota(jnp.int32, (window, LANES), 1)

    def blur(at):
        return at[2] + r1 * (at[1] + at[3]) + r2 * (at[0] + at[4])

    for i in range(count):
        side = i % 2
        p = first_plane + i

        def row(x):
            rows = slice(x * width_y, (x + 1) * width_y)
            return blur([prod[p + k, rows, :] for k in range(5)])

        zero = jnp.zeros((width_y, LANES), F32)
        win = [zero, zero, row(0), row(1)]
        for x in range(width_x):
            win.append(row(x + 2) if x + 2 < width_x else zero)
            pad[side, 8 + x * stride : 8 + x * stride + width_y, :] = blur(win)
            win = win[1:]
        found = []
        for t in range(tiles):
            rows = []
            for x in range(t * per_tile, (t + 1) * per_tile):
                base = 6 + x * stride
                rows.append(blur([pad[side, base + k : base + k + width_y, :] for k in range(5)]))
            value = jnp.concatenate(rows, axis=0)
            high = value.astype(jnp.bfloat16)
            low = (value - high.astype(F32)).astype(jnp.bfloat16)
            number = p * tiles + t
            start = pl.multiple_of((first_ref[number] // 8) * 8, 8)
            voxel = bv_ref[pl.ds(start, window), :]
            hits = []
            for left in range(0, tile, LANES):
                right = min(tile - left, LANES)
                hit = jnp.where(voxel == lane + (left + number * tile), 1.0, 0.0)
                hits.append(hit[:, :right].astype(jnp.bfloat16))
            choose = jnp.concatenate(hits, axis=1)
            both = jnp.concatenate([high, low], axis=1)
            out = jnp.dot(choose, both, preferred_element_type=F32)
            found.append((start, out[:, :LANES] + out[:, LANES:]))
        for start, out in found:
            write(start, out)


def inner_kernel(ratios, shape, planes, tile, near_ref, bv_ref, first_ref, prod, picked, pad):
    odd = lax.axis_index("gz") % 2
    unpack_planes(near_ref, prod, (planes + 2) * (1 - odd), shape[0] * shape[1], NEAR_PARTS, 1.0)
    picked[...] = jnp.zeros_like(picked)

    def write(start, out):
        rest = out.shape[0] - 8
        picked[pl.ds(start, 8), :] += out[:8]
        picked[pl.ds(pl.multiple_of(start + 8, 8), rest), :] = out[8:]

    smooth_and_pick(
        ratios, shape, tile, prod, bv_ref, first_ref, pad, 2 * (1 - odd), planes - 2, write
    )


def inner_rows_kernel(ratios, shape, planes, tile, _, near_ref, bv_ref, first_ref, *refs):
    inner_kernel(ratios, shape, planes, tile, near_ref, bv_ref, first_ref, *refs)


def outer_kernel(
    ratios, shape, planes, tile, share, pieces, carries, *refs
):
    _, far_ref, _, bv_ref, first_ref = refs[:5]
    carried, refs = refs[5 : 5 + carries], refs[5 + carries :]
    prod, picked, refs, pad = refs[0], refs[1], refs[2:-1], refs[-1]
    sends, keeps = refs[: len(pieces)], refs[len(pieces) :]
    g, last = lax.axis_index("gz"), lax.axis_size("gz") - 1
    odd = g % 2
    inside = jnp.where((g == 0) | (g == last), 0.0, 1.0)
    unpack_planes(far_ref, prod, (planes + 2) * odd, shape[0] * shape[1], FAR_PARTS, inside)

    def write(start, out):
        picked[pl.ds(start, out.shape[0]), :] += out

    smooth_and_pick(
        ratios, shape, tile, prod, bv_ref, first_ref, pad, (planes - 2) * odd, 2, write
    )
    mine = lax.axis_index("ta") % 2
    z = lax.axis_index("ta") // 2
    for send, keep, piece in zip(sends, keeps, pieces):
        skip = send.shape[0] - len(piece)
        for k in range(skip):
            send[k] = carried[k][0]
        for k, d in enumerate(piece):
            theirs_at = pl.multiple_of((2 * (z ^ d) + 1 - mine) * share, 8)
            mine_at = pl.multiple_of((2 * (z ^ d) + mine) * share, 8)
            parts = parts_of(send.shape[1], share)
            pack_block(picked[pl.ds(theirs_at, share), :], send.at[skip + k], parts)
            keep[k] = picked[pl.ds(mine_at, share), :]


def parts_of(total, rows):
    parts = (total - rows) // 8
    return parts if rows // parts % 16 == 0 else 1


def unpack_block(block, rows):
    parts = parts_of(block.shape[0], rows)
    scales = unpack_scales(block, rows, parts)
    pieces = [unpack_part(block, rows, part, scales, parts) for part in range(parts)]
    return jnp.concatenate(pieces, axis=0)


def pass_kernel(share, got_ref, keep_ref, out_ref):
    parts = parts_of(out_ref.shape[1], share)
    for k in range(got_ref.shape[0]):
        pack_block(keep_ref[k] + unpack_block(got_ref.at[k], share), out_ref.at[k], parts)


def join_kernel(share, got_ref, keep_ref, near_ref, keep_out, *send_out):
    count = got_ref.shape[0]
    for k in range(count):
        total = keep_ref[k] + unpack_block(got_ref.at[k], share)
        total = total + unpack_block(near_ref.at[k], share)
        if k % 2:
            pack_block(total, send_out[0].at[k // 2], parts_of(send_out[0].shape[1], share))
        else:
            keep_out[k // 2] = total


def fold_kernel(share, got_ref, keep_ref, keep_out, *send_out):
    for k in range(got_ref.shape[0]):
        total = keep_ref[k] + unpack_block(got_ref.at[k], share)
        if k % 2:
            pack_block(total, send_out[0].at[k // 2], parts_of(send_out[0].shape[1], share))
        else:
            keep_out[k // 2] = total


def short_join_kernel(share, got_ref, keep_ref, near_ref, *outs):
    for k, out in enumerate(outs):
        total = keep_ref[k] + unpack_block(got_ref.at[k], share)
        if k == 0:
            total = total + unpack_block(near_ref.at[0], share)
        pack_block(total, out.at[0], parts_of(out.shape[1], share))


def last_kernel(scale, share, chunks, *refs):
    out_ref = refs[-1]
    for c in range(chunks):
        own, got = refs[2 * c : 2 * c + 2]
        value = own[0] + unpack_block(got.at[0], share)
        out_ref[:, c * LANES : (c + 1) * LANES] = value * scale


def column_kernel(scale, share, chunk, side_ref, own, near, far, *refs):
    out_hbm, buf, sem = refs[-3:]
    value = own[0]
    for ref in (side_ref.at[chunk], near.at[0], far.at[0]):
        value = value + unpack_block(ref, share)
    buf[...] = value * scale
    place = out_hbm.at[:, pl.ds(chunk * LANES, LANES)]
    copy = pltpu.make_async_copy(buf, place, sem.at[0])
    copy.start()
    copy.wait()


def shards(volume, sketch_matrix, brain_voxels):
    taps = kernel_taps()
    ratios = (taps[1] / taps[2], taps[0] / taps[2])
    planes, width_x, width_y, time_local = volume.shape
    cells = width_x * width_y
    slab = planes * cells
    rank = sketch_matrix.shape[1]
    chunks = rank // LANES
    picks = brain_voxels.shape[0]
    n_gz, n_ta = lax.axis_size("gz"), lax.axis_size("ta")
    share = picks // n_ta
    blocks = n_ta // 2
    tile = 6 * width_y
    window = tile + 8
    tiles = slab // tile
    vmem = pl.BlockSpec(memory_space=pltpu.VMEM)
    smem = pl.BlockSpec(memory_space=pltpu.SMEM)
    hbm = pl.BlockSpec(memory_space=pltpu.HBM)
    flat = volume.reshape(slab, time_local)

    def message_shapes(which):
        return [
            jax.ShapeDtypeStruct((2, cells + 8 * parts, LANES), I16)
            for c in which
            for parts in (FAR_PARTS, NEAR_PARTS)
        ]

    def packs_of(which, odd):
        top = planes - 2
        return [
            (c, plane, parts)
            for c in which
            for plane, parts in ((top * odd, FAR_PARTS), (top * (1 - odd), NEAR_PARTS))
        ]

    held_shape = jax.ShapeDtypeStruct((planes + 4, cells, LANES), F32)
    picked_shape = jax.ShapeDtypeStruct((picks + window, LANES), F32)
    indices = brain_voxels.reshape(picks // LANES, LANES)
    shapes = message_shapes([0])[:1] + [
        jax.ShapeDtypeStruct((tiles,), jnp.int32),
        jax.ShapeDtypeStruct((picks + window, LANES), jnp.int32),
        jax.ShapeDtypeStruct((time_local, rank), jnp.bfloat16),
    ]
    shapes += [held_shape] * chunks
    out = pl.pallas_call(
        functools.partial(far_kernel, planes, cells, chunks, packs_of),
        out_shape=shapes,
        in_specs=[hbm, hbm, hbm],
        out_specs=[vmem, smem] + [vmem] * (len(shapes) - 2),
        scratch_shapes=[
            pltpu.VMEM((2 * cells, time_local), jnp.bfloat16),
            pltpu.VMEM(indices.shape, jnp.int32),
            pltpu.SemaphoreType.DMA((3,)),
        ],
        compiler_params=VMEM,
        cost_estimate=COST,
        name="far_products",
    )(*[pltpu.with_memory_space_constraint(x, pltpu.HBM) for x in (flat, sketch_matrix, indices)])
    far_message, first, wide, weights = out[:4]
    prods = out[4:]

    def more_products(kernel, shapes, prods, name):
        out = pl.pallas_call(
            functools.partial(kernel, planes, cells, chunks, packs_of),
            out_shape=shapes + [held_shape] * chunks,
            in_specs=[vmem] * (2 + chunks),
            out_specs=[vmem] * (len(shapes) + chunks),
            input_output_aliases={2 + i: len(shapes) + i for i in range(chunks)},
            compiler_params=VMEM,
            cost_estimate=COST,
            name=name,
        )(flat, weights, *prods)
        return list(out[:-chunks]), out[-chunks:]

    near_message, prods = more_products(
        near_kernel, message_shapes([0])[1:], prods, "near_products"
    )
    messages, prods = more_products(
        middle_kernel, message_shapes(range(1, chunks)), prods, "middle_products"
    )
    messages = [far_message] + near_message + messages

    even_pairs = [(i, i ^ 1) for i in range(n_gz)]
    odd_pairs = []
    for i in range(n_gz):
        for j in range(n_ta):
            partner = (i, j ^ 2) if i in (0, n_gz - 1) else (i + 1 if i % 2 else i - 1, j)
            odd_pairs.append((i * n_ta + j, partner[0] * n_ta + partner[1]))

    pad = pltpu.VMEM((2, width_x * (width_y + 8) + 8, LANES), F32)
    short = blocks == 4

    message_of = lambda count: jax.ShapeDtypeStruct((count, share + 16, LANES), I16)
    kept_of = lambda count: jax.ShapeDtypeStruct((count, share, LANES), F32)

    def sums(kernel, shapes, args, name):
        return pl.pallas_call(
            functools.partial(kernel, share),
            out_shape=shapes,
            in_specs=[vmem] * len(args),
            out_specs=[vmem] * len(shapes),
            compiler_params=VMEM,
            cost_estimate=COST,
            name=name,
        )(*args)

    def across(value, mask):
        return lax.ppermute(value, "ta", [(i, i ^ mask) for i in range(n_ta)])

    one, urgent, most_urgent = [
        jax.ShapeDtypeStruct((1, share + extra, LANES), I16) for extra in (16, 32, 48)
    ]

    def finish(near_got, side, kept, before=None):
        shapes = [urgent if before else most_urgent, one]
        far, near = sums(short_join_kernel, shapes, (side[0], kept[0], near_got), "join_sums")
        if before is not None:
            near, before[-2] = lax.optimization_barrier((near, before[-2]))
        return far, [kept[-1], across(near, 2), across(far, 4)]

    results, carried, waiting = [], [], None
    for c in range(chunks):
        near = lax.ppermute(messages[2 * c + 1], "gz", even_pairs)
        far = lax.ppermute(messages[2 * c], ("gz", "ta"), odd_pairs)
        held = prods[c]
        if c:
            held, rows = lax.optimization_barrier((held, rows))
        held, picked = pl.pallas_call(
            functools.partial(inner_rows_kernel, ratios, (width_x, width_y), planes, tile),
            out_shape=[held_shape, picked_shape],
            in_specs=[vmem, vmem, vmem, smem],
            out_specs=[vmem] * 2,
            input_output_aliases={0: 0},
            scratch_shapes=[pad],
            compiler_params=VMEM,
            cost_estimate=COST,
            name="inner_rows",
        )(held, near, wide, first)
        if short:
            pieces = ((3,), (2, 1), (0,))
        else:
            pieces = (range(1, blocks, 2), range(0, blocks, 2))
        counts = [len(piece) for piece in pieces]
        ends = carried if c == chunks - 1 else []
        sent = [message_of(count) for count in counts[:-1]] + [message_of(counts[-1] + len(ends))]
        rows = pl.pallas_call(
            functools.partial(
                outer_kernel, ratios, (width_x, width_y), planes, tile, share, pieces, len(ends)
            ),
            out_shape=[held_shape, picked_shape] + sent + [kept_of(count) for count in counts],
            in_specs=[vmem, vmem, vmem, vmem, smem] + [vmem] * len(ends),
            out_specs=[vmem] * (2 + 2 * len(pieces)),
            input_output_aliases={0: 0, 2: 1},
            scratch_shapes=[pad],
            compiler_params=VMEM,
            cost_estimate=COST,
            name="outer_rows",
        )(held, far, picked, wide, first, *ends)[2:]
        sent, kept = list(rows[: len(pieces)]), rows[len(pieces) :]
        if short:
            done = None
            if waiting:
                waiting[1], *sent = lax.optimization_barrier((waiting[1], *sent))
                (out,) = sums(pass_kernel, [urgent], waiting[:2], "pass_sums")
                out, *sent = lax.optimization_barrier((out, *sent))
                done, result = finish(across(out, 2), *waiting[2:])
                results += result
            side = [across(value, 1) for value in sent[:-1]]
            if done is not None:
                kept = list(kept)
                kept[0], done = lax.optimization_barrier((kept[0], done))
            waiting = [side[0], kept[0], side[1:], kept[1:]]
            carried.append(sent[-1])
            if c == chunks - 1:
                (out,) = sums(pass_kernel, [urgent], waiting[:2], "pass_sums")
                near_got = across(out, 2)
                if results:
                    near_got, results[-1] = lax.optimization_barrier((near_got, results[-1]))
                results += finish(near_got, *waiting[2:], results or None)[1]
                results = [across(sent[-1], 1)] + results
        else:
            side = [across(value, 1) for value in sent]
            (out,) = sums(pass_kernel, [message_of(counts[0])], (side[0], kept[0]), "pass_sums")
            near_got = across(out, 2)
            count, mask = counts[1], 4
            shapes = [kept_of(count // 2), message_of(count // 2)]
            keep, out = sums(join_kernel, shapes, (side[1], kept[1], near_got), "join_sums")
            while count > 2:
                count //= 2
                shapes = [kept_of(count // 2), message_of(count // 2)]
                keep, out = sums(fold_kernel, shapes, (across(out, mask), keep), "fold_sums")
                mask *= 2
            results += [keep, across(out, mask)]

    result = jax.ShapeDtypeStruct((share, rank), F32)
    if short:
        outs = []
        for c in range(chunks):
            args = [results[0]] + results[1 + 3 * c : 4 + 3 * c]
            outs = [
                pl.pallas_call(
                    functools.partial(column_kernel, taps[2] ** 3, share, c),
                    out_shape=result,
                    in_specs=[vmem] * len(args) + [hbm] * len(outs),
                    out_specs=hbm,
                    input_output_aliases={len(args): 0} if outs else {},
                    scratch_shapes=[
                        pltpu.VMEM((share, LANES), F32),
                        pltpu.SemaphoreType.DMA((1,)),
                    ],
                    compiler_params=VMEM,
                    cost_estimate=COST,
                    name="result_columns",
                )(*args, *outs)
            ]
        return outs[0]
    return pl.pallas_call(
        functools.partial(last_kernel, taps[2] ** 3, share, chunks),
        out_shape=result,
        in_specs=[vmem] * len(results),
        out_specs=vmem,
        compiler_params=VMEM,
        name="last_sums",
    )(*results)


def solution(mesh):
    in_specs = (P("gz", None, None, "ta"), P("ta", None), P("gz"))
    out_specs = P(("gz", "ta"), None)
    return jax.shard_map(shards, mesh=mesh, in_specs=in_specs, out_specs=out_specs, check_vma=False)
```
